256 devices in a mesh: ctx: 16 (over z, y_lo), head: 8 (over y_hi, x), dp: 2 (over core).
Axes of the slice: x: 4, y: 4 (y_hi: 2, y_lo: 2; y = y_hi * 2 + y_lo), z: 8, core: 2. Of those that a mesh axis runs over, the one named last changes fastest.
Arguments:
- queries: bfloat16 [4096, 8192], P(('dp', 'ctx'), 'head'), parts along dimension 0, may hold values from -96 to 96
- keys_values: bfloat16 [2, 4096, 512], P(None, ('dp', 'ctx')), parts along dimension 1, may hold values from -4 to 4
- doc_lengths: int32 [16], P('dp'), parts along dimension 0, may hold values from 1 to 1024, 2048 in all
- residual: bfloat16 [4096, 4096], P(('dp', 'ctx', 'head')), parts along dimension 0, may hold values from -3 to 3
- out_weight: bfloat16 [8192, 4096], P('head', 'ctx'), may hold values from -0.25 to 0.25
- norm_gain: float32 [4096], replicated, may hold values from 0.1 to 1.9
- expert_ids: int32 [4096, 8], P(('dp', 'ctx', 'head')), parts along dimension 0, may hold values from 0 to 127, all different within a row; in each aligned block of 16 rows (0 to 15, 16 to 31, ...) at most 2 rows name the same one
- priority: int32 [4096], P(('dp', 'ctx', 'head')), parts along dimension 0, may hold values from 0 to 2047, each once
Outputs:
- hidden: bfloat16 [4096, 4096], P(('dp', 'ctx', 'head')), parts along dimension 0
- expert_rows: bfloat16 [128, 256, 2, 4096], P(('ctx', 'head'), 'dp'), parts along dimension 1
The draws below stay inside these ranges and needn't reach their ends.
There are 2 independent parts, one for each index of `dp`. The reference program is written for one: setup_inputs(seed, part) draws one part's arguments, and reference() takes and returns one part's arrays. A program takes and returns all parts, laid end to end along the dimension named above; an argument that names none is the same for every part. Nothing has to cross between parts.
Inputs may be any that keep to these rules, and one draw needn't show every extreme that they name: `doc_lengths`: the documents lie end to end and fill the pack. `expert_ids`: each token names 8 different experts; the tokens of one block of 16 name one expert at most 2 times. `priority`: each position once.
All inputs are finite; a program needn't handle non-finite values.
Results may differ from the reference program's by a relative error of at most 0.017.
Values may be sent and summed in bfloat16 or wider, within the bound.
A program may use at most 64 MiB of HBM per device.

```python
import math
import jax
import jax.numpy as jnp
import numpy as np
from jax import lax

D = 4096
HEADS = 64
KV_HEADS = 4
HEAD_DIM = 128
TOPK = 8
DOCS = 8
ROWS_DEV = 16
TOKENS = 2048
EXPERTS = 128
CAP = 2


def shared_keys(key):
    return jnp.clip(jax.random.normal(key, (TOKENS, KV_HEADS, HEAD_DIM), jnp.float32), -4.0, 4.0)


def draw_queries(key, part):
    key = jax.random.fold_in(key, 5)
    result = jnp.clip(jax.random.normal(key, (TOKENS, HEADS, HEAD_DIM), jnp.float32), -4.0, 4.0)
    return result.reshape(TOKENS, HEADS * HEAD_DIM).astype(jnp.bfloat16)


def draw_keys_values(key, part):
    base_keys = shared_keys(key)
    key = jax.random.fold_in(key, 9)
    key_rows = base_keys
    value_rows = jnp.clip(jax.random.normal(key, (TOKENS, KV_HEADS, HEAD_DIM), jnp.float32), -4.0, 4.0)
    stacked = jnp.stack([key_rows.reshape(TOKENS, KV_HEADS * HEAD_DIM), value_rows.reshape(TOKENS, KV_HEADS * HEAD_DIM)])
    return stacked.astype(jnp.bfloat16)


def levels(key, dims, pieces, smallest, high):
    loudness = 1.0
    for dim, shards_of in pieces:
        heights = jax.random.uniform(jax.random.fold_in(jax.random.fold_in(key, 6), dim), (shards_of,), jnp.float32, smallest / len(pieces), high / len(pieces))
        loudness = loudness * jnp.repeat(jnp.exp(heights), dims[dim] // shards_of).reshape((-1,) + (1,) * (len(dims) - 1 - dim))
    return loudness


def profile(number_of, total, bound, lean):
    loads = [(1 << 20) // math.isqrt(grade ** lean) + 1 for grade in range(2, number_of + 1)]
    surplus, holding = total - bound - (number_of - 1), [1] * (number_of - 1)
    while surplus > 0:
        free = [i for i in range(number_of - 1) if holding[i] < bound]
        whole, left = sum([loads[i] for i in free]), surplus
        for i in free:
            extra = min(bound - holding[i], max(1, left * loads[i] // whole), surplus)
            holding[i] = holding[i] + extra
            surplus = surplus - extra
    return np.array([bound] + holding)


def uneven_parts(own_key, count, total, most, slope):
    if count == 2:
        one = jax.random.randint(own_key, (), max(1, total - most), min(most, total - 1) + 1)
        return jnp.stack([one, total - one])
    tallies = jnp.asarray(profile(count, total, most, slope), jnp.int32)
    couples = (count - 1) // 2
    source_of, taker = tallies[1:1 + 2 * couples:2], tallies[2:2 + 2 * couples:2]
    room = jnp.minimum(source_of - 1, most - taker)
    passed = jax.random.randint(jax.random.fold_in(own_key, 1), (couples,), 0, 1 << 20) % (room + 1)
    tallies = tallies.at[1:1 + 2 * couples:2].set(source_of - passed).at[2:2 + 2 * couples:2].set(taker + passed)
    return tallies[jax.random.permutation(jax.random.fold_in(own_key, 2), count)]


def shared_out(rng, own, number, rows, amount, top, bound, skew):
    sequence = jax.random.permutation(rng, amount)
    heavy_load, ordinary = load_shares(amount, rows * top, bound, skew, True), load_shares(amount, rows * top, bound, skew, False)
    places = jnp.arange(amount)

    def named(tallies, offset_by):
        used = int((tallies > 0).sum())
        fixed = max(1, used // 4)
        passed = fixed + (places - fixed + offset_by * (used - fixed)) % max(1, amount - fixed)
        return jnp.zeros((amount,), jnp.int32).at[sequence[jnp.where(places < fixed, places, passed)]].set(jnp.asarray(tallies, jnp.int32))

    tallies = jnp.where(number % 4 == 0, named(heavy_load, number // 4), named(ordinary, number - number // 4 - 1))
    mixed = jax.random.permutation(jax.random.fold_in(own, 3), amount)
    giver, taker = mixed[0:amount // 2 * 2:2], mixed[1:amount // 2 * 2:2]
    room = jnp.minimum(tallies[giver] - 1, bound - tallies[taker]) // 2
    room = jnp.where((giver == sequence[0]) | (taker == sequence[0]) | (tallies[taker] == 0), 0, jnp.maximum(room, 0))
    passed = jax.random.randint(jax.random.fold_in(own, 4), (amount // 2,), 0, 1 << 20) % (room + 1)
    tallies = tallies.at[giver].add(-passed).at[taker].add(passed)
    members = jnp.searchsorted(jnp.cumsum(tallies), jnp.arange(rows * top), side="right").astype(jnp.int32)
    listing = members.reshape(top, rows).T
    listing = listing[jax.random.permutation(jax.random.fold_in(own, 1), rows)]
    offset_by = jax.random.randint(jax.random.fold_in(own, 2), (rows, 1), 0, top)
    return jnp.take_along_axis(listing, (jnp.arange(top)[None, :] + offset_by) % top, axis=1)


def load_shares(count, total, reach, lean, full):
    loads = [(1 << 20) // math.isqrt(standing ** lean) + 1 for standing in range(1, count + 1)]
    largest = reach if full else min(reach, max(-(-total // count), total * loads[0] // sum(loads)))
    least = 1 if total - largest >= count - 1 else 0
    counts, rest = [largest] + [least] * (count - 1), total - largest - least * (count - 1)
    while rest > 0:
        free = [i for i in range(1, count) if counts[i] < largest] or [i for i in range(1, count) if counts[i] < reach]
        whole, remaining = sum([loads[i] for i in free]), rest
        for i in free:
            more = min(reach - counts[i], max(1, remaining * loads[i] // whole), rest)
            counts[i] = counts[i] + more
            rest = rest - more
    return np.array(counts)


def scatter_about(rng, dims, spread, most, shards=(), kind=jnp.bfloat16):
    level = levels(rng, dims, shards, -0.22, 0.18) if shards else 1.0
    drawn = jax.random.normal(rng, dims, jnp.float32) * spread * level
    return jnp.minimum(jnp.maximum(drawn, -most), most).astype(kind)


def setup_inputs(seed: int = 0, part: int = 0) -> dict:
    keys = jax.random.split(jax.random.key(seed), 9)
    own_keys = jax.random.split(jax.random.fold_in(keys[8], part), 9)
    queries = draw_queries(jax.random.fold_in(jax.random.fold_in(keys[8], part), 71), part)
    keys_values = draw_keys_values(jax.random.fold_in(jax.random.fold_in(keys[8], part), 71), part)
    doc_lengths = uneven_parts(own_keys[2], DOCS, TOKENS, TOKENS // 2, 2).astype(jnp.int32)
    residual = scatter_about(own_keys[3], (TOKENS, D), 0.5, 3.0, ((0, 128),))
    out_weight = scatter_about(keys[4], (HEADS * HEAD_DIM, D), (KV_HEADS * HEAD_DIM) ** -0.5, 0.25, ((0, 8), (1, 16)))
    norm_gain = jnp.clip(1.0 + 0.18 * jax.random.normal(keys[5], (D,), jnp.float32), 0.1, 1.9)
    expert_ids_keys = jax.random.split(jax.random.fold_in(own_keys[6], 1), TOKENS // ROWS_DEV)
    expert_ids_turns = jax.random.permutation(jax.random.fold_in(own_keys[6], 3), TOKENS // ROWS_DEV)
    expert_ids = jax.vmap(lambda own, number: shared_out(jax.random.fold_in(own_keys[6], 2), own, number, ROWS_DEV, EXPERTS, TOPK, CAP, 2))(expert_ids_keys, expert_ids_turns).reshape((TOKENS, TOPK))
    priority = jax.random.permutation(own_keys[7], TOKENS).astype(jnp.int32)
    return {"queries": queries, "keys_values": keys_values, "doc_lengths": doc_lengths, "residual": residual, "out_weight": out_weight, "norm_gain": norm_gain, "expert_ids": expert_ids, "priority": priority}


def doc_starts(positions, doc_lengths):
    ends = jnp.cumsum(doc_lengths).astype(jnp.int32)
    inside = ends[None, :] <= positions[:, None]
    return lax.optimization_barrier(jnp.sum(jnp.where(inside, doc_lengths[None, :], 0), axis=1)).astype(jnp.int32)

def reference(queries, keys_values, doc_lengths, residual, out_weight, norm_gain, expert_ids, priority):
    positions = jnp.arange(TOKENS, dtype=jnp.int32)
    starts = doc_starts(positions, doc_lengths)
    allowed = (positions[None, :] <= positions[:, None]) & (positions[None, :] >= starts[:, None])
    group_size = HEADS // KV_HEADS
    scale = 1.0 / math.sqrt(HEAD_DIM)
    query_heads = queries.reshape(TOKENS, HEADS, HEAD_DIM).transpose(1, 0, 2)
    key_heads = keys_values[0].reshape(TOKENS, KV_HEADS, HEAD_DIM).transpose(1, 0, 2)
    value_heads = keys_values[1].reshape(TOKENS, KV_HEADS, HEAD_DIM).transpose(1, 0, 2)

    def one_head(inputs):
        query_block, head_number = inputs
        key_block = key_heads[head_number // group_size]
        value_block = value_heads[head_number // group_size]
        scores = jnp.dot(query_block, key_block.T, preferred_element_type=jnp.float32) * scale
        masked = jnp.where(allowed, scores, -jnp.inf)
        highest = lax.optimization_barrier(jnp.max(masked, axis=1, keepdims=True))
        weights = jnp.exp(masked - highest)
        totals = lax.optimization_barrier(jnp.sum(weights, axis=1, keepdims=True))
        mixed = jnp.dot(weights.astype(jnp.bfloat16), value_block, preferred_element_type=jnp.float32) / totals
        return mixed.astype(jnp.bfloat16)
    attended = lax.map(one_head, (query_heads, jnp.arange(HEADS, dtype=jnp.int32)))
    attended = attended.transpose(1, 0, 2).reshape(TOKENS, HEADS * HEAD_DIM)
    projected = jnp.dot(attended, out_weight, preferred_element_type=jnp.float32)
    hidden = (residual.astype(jnp.float32) + projected).astype(jnp.bfloat16)
    hidden_wide = hidden.astype(jnp.float32)
    inverse = lax.rsqrt(lax.optimization_barrier(jnp.mean(hidden_wide * hidden_wide, axis=1, keepdims=True)) + 1e-06)
    normed = (hidden_wide * inverse * norm_gain[None, :]).astype(jnp.bfloat16)
    sources = TOKENS // ROWS_DEV
    block_ids = expert_ids.reshape(sources, ROWS_DEV, TOPK)
    block_order = priority.reshape(sources, ROWS_DEV)
    block_rows = normed.reshape(sources, ROWS_DEV, D)
    expert_range = jnp.arange(EXPERTS, dtype=jnp.int32)
    chosen = lax.optimization_barrier(jnp.sum((block_ids[:, :, :, None] == expert_range[None, None, None, :]).astype(jnp.int32), axis=2))
    earlier = (block_order[:, :, None] < block_order[:, None, :]).astype(jnp.int32)
    ranks = jnp.einsum('bue,but->bte', chosen, earlier)
    slot_range = jnp.arange(CAP, dtype=jnp.int32)

    def one_source(inputs):
        chosen_block, rank_block, row_block = inputs
        selection = (chosen_block.T[:, None, :] == 1) & (rank_block.T[:, None, :] == slot_range[None, :, None])
        placed = jnp.einsum('esr,rd->esd', selection.astype(jnp.float32), row_block.astype(jnp.float32))
        return placed.astype(jnp.bfloat16)
    placed_all = lax.map(one_source, (chosen, ranks, block_rows))
    expert_rows = jnp.swapaxes(placed_all, 0, 1)
    return (hidden, expert_rows)
```

```python
import math

import jax
import jax.numpy as jnp
from jax import lax
from jax.experimental import pallas as pl
from jax.experimental.pallas import tpu as pltpu
from jax.sharding import PartitionSpec as P

D = 4096
HEAD_DIM = 128
HEADS_DEV = 8
ROWS = 128
KV_GROUP = 2
DOCS = 8
TOPK = 8
NZ = 8
PLANE = 16
REACH = 5
CHUNKS = 4
CW = D // CHUNKS
LOW = -1e30
COEF = math.log2(math.e) / math.sqrt(HEAD_DIM)
MESH = pl.DeviceIdType.MESH
OFFSET = (0, -1, -2, -3, 1, 2, 3, 4)
ORDER = (0, 1, 4, 2, 5, 3, 6, 7)


def kernel(
    q_ref, kv_ref, doc_ref, res_ref, w_ref, gain_ref, ids_ref, prio_ref,
    hid_ref, rows_ref,
    qbuf, kvbuf, vext, bias, mx, acc, att, wbuf, mt, mtbuf, sel, psend, prec, xbuf, asend,
    kvu_s, kvu_r, kvy_s, kvy_r, q_s, q_r, w_s, w_r, ws_s, ws_r, mt_s, mt_r,
    p_s, p_r, x_s, x_r, a_s, a_r, l_s,
):
    ctx = lax.axis_index("ctx")
    head = lax.axis_index("head")
    core = lax.axis_index("dp")
    z = ctx // 2
    ylo = ctx % 2
    me = ylo * 8 + head

    def at_z(k):
        return {"ctx": ((z + k + NZ) % NZ) * 2 + ylo}

    def at_plane(p):
        return {"ctx": z * 2 + p // 8, "head": p % 8}

    partner = {"ctx": z * 2 + (1 - ylo)}
    sibling = {"dp": 1 - core}

    def remote(src, dst, s, r, to):
        return pltpu.make_async_remote_copy(
            src_ref=src, dst_ref=dst, send_sem=s, recv_sem=r, device_id=to, device_id_type=MESH
        )

    def wait_for(ref, sem):
        pltpu.make_async_copy(ref, ref, sem).wait()

    barrier = pltpu.get_barrier_semaphore()

    def greet_plane(j, c):
        pl.semaphore_signal(barrier, inc=1, device_id=at_plane((me + j) % PLANE), device_id_type=MESH)
        return c

    def greet_z(j, c):
        pl.semaphore_signal(barrier, inc=1, device_id=at_z(j), device_id_type=MESH)
        return c

    lax.fori_loop(1, PLANE, greet_plane, 0)
    lax.fori_loop(1, NZ, greet_z, 0)
    pl.semaphore_signal(barrier, inc=1, device_id=sibling, device_id_type=MESH)

    key_head = pl.multiple_of((head // KV_GROUP) * HEAD_DIM, HEAD_DIM)
    for i in range(2):
        kvbuf[0, i, ylo] = kv_ref[i, :, pl.ds(key_head, HEAD_DIM)]
    qbuf[ylo] = q_ref[...]

    row16 = lax.broadcasted_iota(jnp.int32, (16, 128), 0)
    lane16 = lax.broadcasted_iota(jnp.int32, (16, 128), 1)
    chosen = jnp.zeros((16, 128), jnp.float32)
    for k in range(TOPK):
        chosen = chosen + jnp.where(ids_ref[:, k : k + 1] == lane16, 1.0, 0.0)
    prio_row = jnp.full((16, 128), 1 << 20, jnp.int32)
    prio_col = jnp.zeros((16, 128), jnp.int32)
    for u in range(16):
        prio_row = jnp.where(lane16 == u, prio_ref[u], prio_row)
        prio_col = jnp.where(row16 == u, prio_ref[u], prio_col)
    earlier = jnp.where((prio_row < prio_col) & (lane16 < 16), 1.0, 0.0)[:, :16]
    ranks = jnp.dot(
        earlier.astype(jnp.bfloat16), chosen.astype(jnp.bfloat16), preferred_element_type=jnp.float32
    )
    slots = jnp.where(chosen > 0.5, ranks + 1.0, 0.0)
    place = jnp.where(lane16 == row16 + 16 * z, 1.0, 0.0)
    mt[...] = lax.dot_general(
        slots.astype(jnp.bfloat16),
        place.astype(jnp.bfloat16),
        (((0,), (0,)), ((), ())),
        preferred_element_type=jnp.float32,
    )

    pl.semaphore_wait(barrier, PLANE - 1 + NZ - 1 + 1)

    half = pl.ds(pl.multiple_of(core * 512, 512), 512)

    def kv_up(r):
        return remote(kvbuf.at[r - 1, :, ylo], kvbuf.at[r, :, ylo], kvu_s.at[r], kvu_r.at[r], at_z(1))

    def kv_side(r):
        return remote(kvbuf.at[r, :, ylo], kvbuf.at[r, :, ylo], kvy_s.at[r], kvy_r.at[r], partner)

    def w_ring(s):
        first = s in (1, 4)
        src = w_ref.at[half, :] if first else wbuf.at[s - 1, half, :]
        return remote(src, wbuf.at[s, half, :], w_s.at[s], w_r.at[s], at_z(1 if s < 4 else -1))

    def w_side(s):
        return remote(wbuf.at[s, half, :], wbuf.at[s, half, :], ws_s.at[s], ws_r.at[s], sibling)

    q_swap = remote(qbuf.at[ylo], qbuf.at[ylo], q_s, q_r, partner)
    kv_up(1).start()
    kv_side(0).start()
    w_ring(4).start()
    w_ring(1).start()
    q_swap.start()

    def mt_copy(j):
        to = (z + j) % NZ
        rows = pl.ds(pl.multiple_of(to * 16, 16), 16)
        return remote(mt.at[rows, :], mtbuf.at[z], mt_s, mt_r, at_z(j))

    def mt_send(j, c):
        mt_copy(j).start()
        return c

    lax.fori_loop(1, NZ, mt_send, 0)
    mtbuf[z] = mt[pl.ds(pl.multiple_of(z * 16, 16), 16), :]

    def w_forward(s):
        remote_in = w_ring(s)
        remote_in.wait_recv()
        if s not in (3, 7):
            w_ring(s + 1).start()
        w_side(s).start()

    vext[:, HEAD_DIM:] = jnp.ones((2 * ROWS, HEAD_DIM), jnp.bfloat16)
    row = lax.broadcasted_iota(jnp.int32, (ROWS, 2 * ROWS), 0)
    lane = lax.broadcasted_iota(jnp.int32, (ROWS, 2 * ROWS), 1)

    def attend(r, yq):
        key_pos = ((z - r + NZ) % NZ) * 256 + lane
        pos = (2 * z + yq) * ROWS + row
        start = jnp.zeros((ROWS, 2 * ROWS), jnp.int32)
        end = jnp.int32(0)
        for d in range(DOCS):
            length = doc_ref[d]
            end = end + length
            start = start + jnp.where(pos >= end, length, 0)
        bias[...] = jnp.where((key_pos <= pos) & (key_pos >= start), 0.0, LOW)
        vext[:, :HEAD_DIM] = kvbuf[r, 1].reshape(2 * ROWS, HEAD_DIM)

        def one(h, c):
            b = yq * HEADS_DEV + h
            cols = pl.ds(pl.multiple_of(h * HEAD_DIM, HEAD_DIM), HEAD_DIM)
            s = lax.dot_general(
                qbuf[yq, :, cols],
                kvbuf[r, 0].reshape(2 * ROWS, HEAD_DIM),
                (((1,), (1,)), ((), ())),
                preferred_element_type=jnp.float32,
            )
            s = s + bias[...]
            top = jnp.max(s, axis=1, keepdims=True)
            if r > 0:
                old = mx[b]
                new = jnp.maximum(old, top)
            else:
                new = jnp.broadcast_to(top, (ROWS, HEAD_DIM))
            wide = jnp.concatenate([new, new], axis=1)
            weight = jnp.exp2((s - wide) * COEF).astype(jnp.bfloat16)
            out = jnp.dot(weight, vext[...], preferred_element_type=jnp.float32)
            if r > 0:
                factor = jnp.exp2((old - new) * COEF)
                out = out + acc[b] * jnp.concatenate([factor, factor], axis=1)
            if r < REACH - 1:
                mx[b] = new
                acc[b] = out
            else:
                rows = pl.ds(pl.multiple_of(yq * ROWS, ROWS), ROWS)
                att[rows, cols] = (out[:, :HEAD_DIM] / out[:, HEAD_DIM:]).astype(jnp.bfloat16)
            return c

        lax.fori_loop(0, HEADS_DEV, one, 0)

    def kv_step(r):
        kv_up(r).wait_recv()
        if r < REACH - 1:
            kv_up(r + 1).start()
        kv_side(r).start()
        kv_side(r).wait_recv()

    kv_side(0).wait_recv()
    attend(0, ylo)
    kv_step(1)
    attend(1, ylo)
    kv_step(2)
    attend(2, ylo)
    w_forward(4)
    w_forward(1)
    kv_step(3)
    attend(3, ylo)
    q_swap.wait_recv()
    attend(0, 1 - ylo)
    attend(1, 1 - ylo)
    attend(2, 1 - ylo)
    w_forward(5)
    w_forward(2)
    attend(3, 1 - ylo)
    kv_step(4)
    attend(4, ylo)
    attend(4, 1 - ylo)

    def p_copy(o, j):
        to = (me + j) % PLANE
        rows = pl.ds(pl.multiple_of(to * 16, 16), 16)
        return remote(psend.at[o, rows, :], prec.at[o, me], p_s.at[o], p_r.at[o], at_plane(to))

    def project(o):
        if o == 0:
            part = jnp.dot(att[...], w_ref[...], preferred_element_type=jnp.float32)
        else:
            w_side(o).wait_recv()
            part = jnp.dot(att[...], wbuf[o], preferred_element_type=jnp.float32)
        psend[o] = part.astype(jnp.bfloat16)
        prec[o, me] = psend[o, pl.ds(pl.multiple_of(me * 16, 16), 16), :]

        def send(j, c):
            p_copy(o, j).start()
            return c

        lax.fori_loop(1, PLANE, send, 0)

    project(0)
    project(4)
    project(1)
    w_forward(6)
    w_forward(3)
    project(5)
    project(2)
    w_forward(7)
    project(6)
    project(3)
    project(7)

    wait_for(mtbuf.at[pl.ds(0, NZ - 1)], mt_r)
    table = mtbuf[0]
    for i in range(1, NZ):
        table = table + mtbuf[i]
    want = jnp.where(lane16 // 16 == row16 // 2, (row16 % 2 + 1).astype(jnp.float32), -1.0)
    for d in range(PLANE):
        hit = jnp.broadcast_to(table[d : d + 1, :], (16, 128)) == want
        sel[pl.ds(d * 16, 16), :] = jnp.where(hit, 1.0, 0.0).astype(jnp.bfloat16)

    squares = jnp.zeros((16, 1), jnp.float32)
    for o in ORDER:
        wait_for(prec.at[o, pl.ds(0, PLANE - 1)], p_r.at[o])
        for side in range(2):
            total = jnp.zeros((16, 256), jnp.float32)
            for h in range(8):
                total = total + prec[o, side * 8 + h].astype(jnp.float32)
            first = ((z + OFFSET[o] + NZ) % NZ) * 2 + side
            cols = pl.ds(pl.multiple_of(first * 256, 256), 256)
            hidden = (res_ref[:, cols].astype(jnp.float32) + total).astype(jnp.bfloat16)
            hid_ref[:, cols] = hidden
            wide = hidden.astype(jnp.float32)
            squares = squares + jnp.sum(wide * wide, axis=1, keepdims=True)
    inverse = lax.rsqrt(squares / D + 1e-06)

    def x_copy(g, j):
        cols = pl.ds(g * CW, CW)
        return remote(xbuf.at[z, :, cols], xbuf.at[z, :, cols], x_s.at[g], x_r.at[g], at_z(j))

    for g in range(CHUNKS):
        cols = slice(g * CW, (g + 1) * CW)
        normed = hid_ref[:, cols].astype(jnp.float32) * inverse * gain_ref[:, cols]
        xbuf[z, :, cols] = normed.astype(jnp.bfloat16)

        def send_x(j, c, g=g):
            x_copy(g, j).start()
            return c

        lax.fori_loop(1, NZ, send_x, 0)

    def a_copy(g, j):
        to = (me + j) % PLANE
        cols = pl.ds(g * CW, CW)
        return remote(asend.at[to, :, cols], rows_ref.at[me, :, cols], a_s.at[g], a_r.at[g], at_plane(to))

    def own_copy(g):
        cols = pl.ds(g * CW, CW)
        return pltpu.make_async_copy(asend.at[me, :, cols], rows_ref.at[me, :, cols], l_s.at[g])

    for g in range(CHUNKS):
        cols = slice(g * CW, (g + 1) * CW)
        wait_for(xbuf.at[pl.ds(0, NZ - 1), :, pl.ds(g * CW, CW)], x_r.at[g])
        gathered = xbuf[:, :, cols].reshape(ROWS, CW)
        picked = jnp.dot(sel[...], gathered, preferred_element_type=jnp.float32)
        asend[:, :, cols] = picked.astype(jnp.bfloat16).reshape(PLANE, 16, CW)

        def send_a(j, c, g=g):
            a_copy(g, j).start()
            return c

        lax.fori_loop(1, PLANE, send_a, 0)
        own_copy(g).start()

    for r in range(1, REACH):
        kv_up(r).wait_send()
    for r in range(REACH):
        kv_side(r).wait_send()
    q_swap.wait_send()
    for s in range(1, NZ):
        w_ring(s).wait_send()
        w_side(s).wait_send()
    wait_for(mtbuf.at[pl.ds(0, NZ - 1)], mt_s)
    for o in range(NZ):
        wait_for(prec.at[o, pl.ds(0, PLANE - 1)], p_s.at[o])
    for g in range(CHUNKS):
        wait_for(xbuf.at[pl.ds(0, NZ - 1), :, pl.ds(g * CW, CW)], x_s.at[g])
        wait_for(asend.at[pl.ds(0, PLANE - 1), :, pl.ds(g * CW, CW)], a_s.at[g])
        own_copy(g).wait()
    for g in range(CHUNKS):
        wait_for(asend.at[pl.ds(0, PLANE - 1), :, pl.ds(g * CW, CW)], a_r.at[g])


def local(queries, keys_values, doc_lengths, residual, out_weight, norm_gain, expert_ids, priority):
    vmem = pl.BlockSpec(memory_space=pltpu.VMEM)
    smem = pl.BlockSpec(memory_space=pltpu.SMEM)
    bf16, f32 = jnp.bfloat16, jnp.float32
    dma = pltpu.SemaphoreType.DMA
    hidden, rows = pl.pallas_call(
        kernel,
        out_shape=(
            jax.ShapeDtypeStruct((16, D), bf16),
            jax.ShapeDtypeStruct((PLANE, 16, D), bf16),
        ),
        in_specs=[vmem, vmem, smem, vmem, vmem, vmem, vmem, smem],
        out_specs=(vmem, pl.BlockSpec(memory_space=pl.ANY)),
        scratch_shapes=[
            pltpu.VMEM((2, ROWS, 1024), bf16),
            pltpu.VMEM((REACH, 2, 2, ROWS, HEAD_DIM), bf16),
            pltpu.VMEM((2 * ROWS, 2 * HEAD_DIM), bf16),
            pltpu.VMEM((ROWS, 2 * ROWS), f32),
            pltpu.VMEM((16, ROWS, HEAD_DIM), f32),
            pltpu.VMEM((16, ROWS, 2 * HEAD_DIM), f32),
            pltpu.VMEM((2 * ROWS, 1024), bf16),
            pltpu.VMEM((NZ, 1024, 256), bf16),
            pltpu.VMEM((128, 128), f32),
            pltpu.VMEM((NZ, 16, 128), f32),
            pltpu.VMEM((256, 128), bf16),
            pltpu.VMEM((NZ, 256, 256), bf16),
            pltpu.VMEM((NZ, PLANE, 16, 256), bf16),
            pltpu.VMEM((NZ, 16, D), bf16),
            pltpu.VMEM((PLANE, 16, D), bf16),
            dma((REACH,)), dma((REACH,)), dma((REACH,)), dma((REACH,)),
            dma(()), dma(()),
            dma((NZ,)), dma((NZ,)), dma((NZ,)), dma((NZ,)),
            dma(()), dma(()),
            dma((NZ,)), dma((NZ,)),
            dma((CHUNKS,)), dma((CHUNKS,)), dma((CHUNKS,)), dma((CHUNKS,)), dma((CHUNKS,)),
        ],
        compiler_params=pltpu.CompilerParams(
            collective_id=0, has_side_effects=True, vmem_limit_bytes=48 * 1024 * 1024
        ),
    )(
        queries, keys_values, doc_lengths, residual, out_weight,
        norm_gain.reshape(1, D), expert_ids, priority,
    )
    rows = rows.reshape(PLANE, NZ, 2, D).transpose(1, 0, 2, 3).reshape(1, PLANE * NZ, 2, D)
    return hidden, rows


def solution(mesh):
    return jax.shard_map(
        local,
        mesh=mesh,
        in_specs=(
            P(("dp", "ctx"), "head"),
            P(None, ("dp", "ctx"), None),
            P("dp"),
            P(("dp", "ctx", "head"), None),
            P("head", "ctx"),
            P(),
            P(("dp", "ctx", "head"), None),
            P(("dp", "ctx", "head")),
        ),
        out_specs=(P(("dp", "ctx", "head"), None), P(("ctx", "head"), "dp", None, None)),
        check_vma=False,
    )
```

```python
import math

import jax
import jax.numpy as jnp
from jax import lax
from jax.experimental import pallas as pl
from jax.experimental.pallas import tpu as pltpu
from jax.sharding import PartitionSpec as P

D = 4096
HEAD_DIM = 128
HEADS_DEV = 8
ROWS = 128
KV_GROUP = 2
DOCS = 8
TOPK = 8
NZ = 8
PLANE = 16
REACH = 5
CHUNKS = 4
CW = D // CHUNKS
WCH = 2
WROWS = 512 // WCH
LOW = -1e30
COEF = math.log2(math.e) / math.sqrt(HEAD_DIM)
MESH = pl.DeviceIdType.MESH
OFFSET = (0, -1, -2, -3, 1, 2, 3, 4)
ORDER = (0, 1, 4, 2, 5, 3, 6, 7)


def kernel(
    q_ref, kv_ref, doc_ref, res_ref, w_ref, gain_ref, ids_ref, prio_ref,
    hid_ref, rows_ref,
    qbuf, kvbuf, vt, mx, acc, att, wbuf, res, gain, ids, prio, docs, mt, mtbuf, sel, psend, prec,
    xbuf, asend,
    in_s, kvu_s, kvu_r, kvy_s, kvy_r, q_s, q_r, w_s, w_r, ws_s, ws_r, mt_s, mt_r,
    p_s, p_r, x_s, x_r, a_s, a_r, l_s,
):
    ctx = lax.axis_index("ctx")
    head = lax.axis_index("head")
    core = lax.axis_index("dp")
    z = ctx // 2
    ylo = ctx % 2
    me = ylo * 8 + head

    def at_z(k):
        return {"ctx": ((z + k + NZ) % NZ) * 2 + ylo}

    def at_plane(p):
        return {"ctx": z * 2 + p // 8, "head": p % 8}

    partner = {"ctx": z * 2 + (1 - ylo)}
    sibling = {"dp": 1 - core}

    def remote(src, dst, s, r, to):
        return pltpu.make_async_remote_copy(
            src_ref=src, dst_ref=dst, send_sem=s, recv_sem=r, device_id=to, device_id_type=MESH
        )

    def wait_for(ref, sem):
        pltpu.make_async_copy(ref, ref, sem).wait()

    key_head = pl.multiple_of((head // KV_GROUP) * HEAD_DIM, HEAD_DIM)
    loads = [
        pltpu.make_async_copy(src, dst, in_s.at[i])
        for i, (src, dst) in enumerate(
            (
                (kv_ref.at[:, :, pl.ds(key_head, HEAD_DIM)], kvbuf.at[0, :, ylo]),
                (q_ref, qbuf.at[ylo]),
                (w_ref, wbuf.at[0]),
                (ids_ref, ids),
                (prio_ref, prio),
                (doc_ref, docs),
                (res_ref, res),
                (gain_ref, gain),
            )
        )
    ]
    for copy in loads:
        copy.start()

    barrier = pltpu.get_barrier_semaphore()

    def greet_plane(j, c):
        pl.semaphore_signal(barrier, inc=1, device_id=at_plane((me + j) % PLANE), device_id_type=MESH)
        return c

    def greet_z(j, c):
        pl.semaphore_signal(barrier, inc=1, device_id=at_z(j), device_id_type=MESH)
        return c

    lax.fori_loop(1, PLANE, greet_plane, 0)
    lax.fori_loop(1, NZ, greet_z, 0)
    pl.semaphore_signal(barrier, inc=1, device_id=sibling, device_id_type=MESH)

    def make_slots():
        row16 = lax.broadcasted_iota(jnp.int32, (16, 128), 0)
        lane16 = lax.broadcasted_iota(jnp.int32, (16, 128), 1)
        expert = lax.broadcasted_iota(jnp.int32, (128, 16), 0)
        chosen = jnp.zeros((128, 16), jnp.float32)
        for k in range(TOPK):
            chosen = chosen + jnp.where(ids[k : k + 1, :] == expert, 1.0, 0.0)
        prio_row = jnp.zeros((16, 128), jnp.int32)
        prio_col = jnp.zeros((16, 128), jnp.int32)
        for u in range(16):
            prio_row = jnp.where(lane16 == u, prio[u], prio_row)
            prio_col = jnp.where(row16 == u, prio[u], prio_col)
        earlier = jnp.where(prio_col < prio_row, 1.0, 0.0)[:, :16]
        ranks = jnp.dot(
            chosen.astype(jnp.bfloat16), earlier.astype(jnp.bfloat16), preferred_element_type=jnp.float32
        )
        slots = jnp.where(chosen > 0.5, ranks + 1.0, 0.0)
        place = jnp.where(lane16 == row16 + 16 * z, 1.0, 0.0)
        mt[...] = jnp.dot(
            slots.astype(jnp.bfloat16), place.astype(jnp.bfloat16), preferred_element_type=jnp.float32
        )

    pl.semaphore_wait(barrier, PLANE - 1 + NZ - 1 + 1)

    def kv_up(r):
        return remote(kvbuf.at[r - 1, :, ylo], kvbuf.at[r, :, ylo], kvu_s.at[r], kvu_r.at[r], at_z(1))

    def kv_side(r):
        return remote(kvbuf.at[r, :, ylo], kvbuf.at[r, :, ylo], kvy_s.at[r], kvy_r.at[r], partner)

    def w_rows(c):
        return pl.ds(pl.multiple_of(core * 512 + c * WROWS, WROWS), WROWS)

    def w_ring(s, c):
        src = w_ref.at[w_rows(c), :] if s in (1, 4) else wbuf.at[s - 1, w_rows(c), :]
        to = at_z(1 if s < 4 else -1)
        return remote(src, wbuf.at[s, w_rows(c), :], w_s.at[s, c], w_r.at[s, c], to)

    def w_side(s, c):
        part = wbuf.at[s, w_rows(c), :]
        return remote(part, part, ws_s.at[s, c], ws_r.at[s, c], sibling)

    def w_forward(s):
        for c in range(WCH):
            w_ring(s, c).wait_recv()
            if s not in (3, 7):
                w_ring(s + 1, c).start()
            w_side(s, c).start()

    q_swap = remote(qbuf.at[ylo], qbuf.at[ylo], q_s, q_r, partner)
    for c in range(WCH):
        w_ring(4, c).start()
    loads[0].wait()
    kv_up(1).start()
    kv_side(0).start()
    loads[1].wait()
    q_swap.start()
    for copy in loads[3:]:
        copy.wait()
    make_slots()

    def mt_copy(j):
        to = (z + j) % NZ
        rows = pl.ds(pl.multiple_of(to * 16, 16), 16)
        return remote(mt.at[rows, :], mtbuf.at[z], mt_s, mt_r, at_z(j))

    def mt_send(j, c):
        mt_copy(j).start()
        return c

    lax.fori_loop(1, NZ, mt_send, 0)
    mtbuf[z] = mt[pl.ds(pl.multiple_of(z * 16, 16), 16), :]

    vt[HEAD_DIM:, :] = jnp.ones((16, 2 * ROWS), jnp.bfloat16)
    row = lax.broadcasted_iota(jnp.int32, (2 * ROWS, ROWS), 0)
    lane = lax.broadcasted_iota(jnp.int32, (1, ROWS), 1)

    def attend(r, yq):
        key_pos = ((z - r + NZ) % NZ) * 256 + row
        pos = (2 * z + yq) * ROWS + lane
        start = jnp.zeros((1, ROWS), jnp.int32)
        end = jnp.int32(0)
        for d in range(DOCS):
            length = docs[d]
            end = end + length
            start = start + jnp.where(pos >= end, length, 0)
        bias = jnp.where((key_pos <= pos) & (key_pos >= start), 0.0, LOW)
        bias = jnp.concatenate([bias, bias], axis=1)
        keys = kvbuf[r, 0].reshape(2 * ROWS, HEAD_DIM)
        vt[:HEAD_DIM, :] = kvbuf[r, 1].reshape(2 * ROWS, HEAD_DIM).T
        for pair in range(HEADS_DEV // 2):
            b = yq * (HEADS_DEV // 2) + pair
            first = pair * 2 * HEAD_DIM
            query = jnp.concatenate(
                [
                    qbuf[yq, :, first : first + HEAD_DIM],
                    qbuf[yq, :, first + HEAD_DIM : first + 2 * HEAD_DIM],
                ],
                axis=0,
            )
            s = lax.dot_general(
                keys, query, (((1,), (1,)), ((), ())), preferred_element_type=jnp.float32
            )
            s = s + bias
            new = jnp.max(s, axis=0, keepdims=True)
            if r > 0:
                old = mx[b]
                new = jnp.maximum(old, new)
            weight = jnp.exp2((s - new) * COEF).astype(jnp.bfloat16)
            out = jnp.dot(vt[...], weight, preferred_element_type=jnp.float32)
            if r > 0:
                out = out + acc[b] * jnp.exp2((old - new) * COEF)
            if r < REACH - 1:
                mx[b] = new
                acc[b] = out
            else:
                mixed = out[:HEAD_DIM] / out[HEAD_DIM : HEAD_DIM + 1]
                rows = pl.ds(pl.multiple_of(yq * ROWS, ROWS), ROWS)
                for i in range(2):
                    one = mixed[:, i * ROWS : (i + 1) * ROWS].T.astype(jnp.bfloat16)
                    att[rows, first + i * HEAD_DIM : first + (i + 1) * HEAD_DIM] = one

    def kv_step(r):
        kv_up(r).wait_recv()
        if r < REACH - 1:
            kv_up(r + 1).start()
        kv_side(r).start()

    kv_step(1)
    kv_side(0).wait_recv()
    attend(0, ylo)
    kv_step(2)
    for c in range(WCH):
        w_ring(1, c).start()
    kv_side(1).wait_recv()
    attend(1, ylo)
    kv_step(3)
    w_forward(4)
    kv_side(2).wait_recv()
    attend(2, ylo)
    kv_step(4)
    q_swap.wait_recv()
    attend(0, 1 - ylo)
    attend(1, 1 - ylo)
    attend(2, 1 - ylo)
    w_forward(1)
    kv_side(3).wait_recv()
    attend(3, ylo)
    attend(3, 1 - ylo)
    w_forward(5)
    kv_side(4).wait_recv()
    attend(4, ylo)
    attend(4, 1 - ylo)

    def p_copy(o, j):
        to = (me + j) % PLANE
        rows = pl.ds(pl.multiple_of(to * 16, 16), 16)
        return remote(psend.at[o, rows, :], prec.at[o, me], p_s.at[o], p_r.at[o], at_plane(to))

    def project(o):
        if o == 0:
            loads[2].wait()
        else:
            for c in range(WCH):
                w_side(o, c).wait_recv()
        part = jnp.dot(att[...], wbuf[o], preferred_element_type=jnp.float32)
        psend[o] = part.astype(jnp.bfloat16)
        prec[o, me] = psend[o, pl.ds(pl.multiple_of(me * 16, 16), 16), :]

        def send(j, c):
            p_copy(o, j).start()
            return c

        lax.fori_loop(1, PLANE, send, 0)

    project(0)
    project(4)
    w_forward(2)
    project(1)
    w_forward(6)
    project(5)
    project(2)
    w_forward(3)
    w_forward(7)
    project(6)
    project(3)
    project(7)

    row16 = lax.broadcasted_iota(jnp.int32, (16, 128), 0)
    lane16 = lax.broadcasted_iota(jnp.int32, (16, 128), 1)
    wait_for(mtbuf.at[pl.ds(0, NZ - 1)], mt_r)
    table = mtbuf[0]
    for i in range(1, NZ):
        table = table + mtbuf[i]
    want = jnp.where(lane16 // 16 == row16 // 2, (row16 % 2 + 1).astype(jnp.float32), -1.0)
    for d in range(PLANE):
        hit = jnp.broadcast_to(table[d : d + 1, :], (16, 128)) == want
        sel[pl.ds(d * 16, 16), :] = jnp.where(hit, 1.0, 0.0).astype(jnp.bfloat16)

    squares = jnp.zeros((16, 1), jnp.float32)
    for o in ORDER:
        wait_for(prec.at[o, pl.ds(0, PLANE - 1)], p_r.at[o])
        for side in range(2):
            total = jnp.zeros((16, 256), jnp.float32)
            for h in range(8):
                total = total + prec[o, side * 8 + h].astype(jnp.float32)
            first = ((z + OFFSET[o] + NZ) % NZ) * 2 + side
            cols = pl.ds(pl.multiple_of(first * 256, 256), 256)
            hidden = (res[:, cols].astype(jnp.float32) + total).astype(jnp.bfloat16)
            hid_ref[:, cols] = hidden
            wide = hidden.astype(jnp.float32)
            squares = squares + jnp.sum(wide * wide, axis=1, keepdims=True)
    inverse = lax.rsqrt(squares / D + 1e-06)

    for g in range(CHUNKS):
        cols = slice(g * CW, (g + 1) * CW)
        normed = hid_ref[:, cols].astype(jnp.float32) * inverse * gain[:, cols]
        xbuf[z, :, cols] = normed.astype(jnp.bfloat16)

    def x_hops(g, way):
        return 4 if g % 2 == way else 3

    def x_ring(g, way, r):
        part = xbuf.at[(z + (1 - r if way == 0 else r - 1) + NZ) % NZ, :, pl.ds(g * CW, CW)]
        return remote(part, part, x_s.at[way, g, r], x_r.at[way, g, r], at_z(1 if way == 0 else -1))

    def a_copy(g, j):
        to = (me + j) % PLANE
        cols = pl.ds(g * CW, CW)
        return remote(
            asend.at[to, :, :, cols], rows_ref.at[:, me, :, cols], a_s.at[g], a_r.at[g], at_plane(to)
        )

    def own_copy(g):
        cols = pl.ds(g * CW, CW)
        return pltpu.make_async_copy(asend.at[me, :, :, cols], rows_ref.at[:, me, :, cols], l_s.at[g])

    for t in range(2 * (CHUNKS - 1) + 5):
        for g in range(CHUNKS):
            r = t - 2 * g
            for way in range(2):
                if 1 <= r <= x_hops(g, way):
                    x_ring(g, way, r).wait_recv()
                if 0 <= r < x_hops(g, way):
                    x_ring(g, way, r + 1).start()
            if r == 4:
                cols = slice(g * CW, (g + 1) * CW)
                gathered = xbuf[:, :, cols].reshape(ROWS, CW)
                picked = jnp.dot(sel[...], gathered, preferred_element_type=jnp.float32)
                asend[:, :, :, cols] = picked.astype(jnp.bfloat16).reshape(PLANE, NZ, 2, CW)

                def send_a(j, c, g=g):
                    a_copy(g, j).start()
                    return c

                lax.fori_loop(1, PLANE, send_a, 0)
                own_copy(g).start()

    for r in range(1, REACH):
        kv_up(r).wait_send()
    for r in range(REACH):
        kv_side(r).wait_send()
    q_swap.wait_send()
    for s in range(1, NZ):
        for c in range(WCH):
            w_ring(s, c).wait_send()
            w_side(s, c).wait_send()
    wait_for(mtbuf.at[pl.ds(0, NZ - 1)], mt_s)
    for o in range(NZ):
        wait_for(prec.at[o, pl.ds(0, PLANE - 1)], p_s.at[o])
    for g in range(CHUNKS):
        for way in range(2):
            for r in range(1, x_hops(g, way) + 1):
                x_ring(g, way, r).wait_send()
        wait_for(asend.at[pl.ds(0, PLANE - 1), :, :, pl.ds(g * CW, CW)], a_s.at[g])
        own_copy(g).wait()
    for g in range(CHUNKS):
        wait_for(asend.at[pl.ds(0, PLANE - 1), :, :, pl.ds(g * CW, CW)], a_r.at[g])


def local(queries, keys_values, doc_lengths, residual, out_weight, norm_gain, expert_ids, priority):
    anywhere = pl.BlockSpec(memory_space=pl.ANY)
    bf16, f32 = jnp.bfloat16, jnp.float32
    dma = pltpu.SemaphoreType.DMA
    hidden, rows = pl.pallas_call(
        kernel,
        out_shape=(
            jax.ShapeDtypeStruct((16, D), bf16),
            jax.ShapeDtypeStruct((NZ, PLANE, 2, D), bf16),
        ),
        in_specs=[anywhere] * 8,
        out_specs=(pl.BlockSpec(memory_space=pltpu.VMEM), anywhere),
        scratch_shapes=[
            pltpu.VMEM((2, ROWS, 1024), bf16),
            pltpu.VMEM((REACH, 2, 2, ROWS, HEAD_DIM), bf16),
            pltpu.VMEM((HEAD_DIM + 16, 2 * ROWS), bf16),
            pltpu.VMEM((HEADS_DEV, 1, 2 * ROWS), f32),
            pltpu.VMEM((HEADS_DEV, HEAD_DIM + 16, 2 * ROWS), f32),
            pltpu.VMEM((2 * ROWS, 1024), bf16),
            pltpu.VMEM((NZ, 1024, 256), bf16),
            pltpu.VMEM((16, D), bf16),
            pltpu.VMEM((1, D), f32),
            pltpu.VMEM((TOPK, 16), jnp.int32),
            pltpu.SMEM((16,), jnp.int32),
            pltpu.SMEM((DOCS,), jnp.int32),
            pltpu.VMEM((128, 128), f32),
            pltpu.VMEM((NZ, 16, 128), f32),
            pltpu.VMEM((256, 128), bf16),
            pltpu.VMEM((NZ, 256, 256), bf16),
            pltpu.VMEM((NZ, PLANE, 16, 256), bf16),
            pltpu.VMEM((NZ, 16, D), bf16),
            pltpu.VMEM((PLANE, NZ, 2, D), bf16),
            dma((8,)),
            dma((REACH,)), dma((REACH,)), dma((REACH,)), dma((REACH,)),
            dma(()), dma(()),
            dma((NZ, WCH)), dma((NZ, WCH)), dma((NZ, WCH)), dma((NZ, WCH)),
            dma(()), dma(()),
            dma((NZ,)), dma((NZ,)),
            dma((2, CHUNKS, 5)), dma((2, CHUNKS, 5)),
            dma((CHUNKS,)), dma((CHUNKS,)), dma((CHUNKS,)),
        ],
        compiler_params=pltpu.CompilerParams(
            collective_id=0, has_side_effects=True, vmem_limit_bytes=60 * 1024 * 1024
        ),
    )(
        queries, keys_values, doc_lengths, residual, out_weight,
        norm_gain.reshape(1, D), expert_ids.T, priority,
    )
    return hidden, rows.reshape(1, PLANE * NZ, 2, D)


def solution(mesh):
    return jax.shard_map(
        local,
        mesh=mesh,
        in_specs=(
            P(("dp", "ctx"), "head"),
            P(None, ("dp", "ctx"), None),
            P("dp"),
            P(("dp", "ctx", "head"), None),
            P("head", "ctx"),
            P(),
            P(("dp", "ctx", "head"), None),
            P(("dp", "ctx", "head")),
        ),
        out_specs=(P(("dp", "ctx", "head"), None), P(("ctx", "head"), "dp", None, None)),
        check_vma=False,
    )
```

```python
import math

import jax
import jax.numpy as jnp
from jax import lax
from jax.experimental import pallas as pl
from jax.experimental.pallas import tpu as pltpu
from jax.sharding import PartitionSpec as P

D = 4096
HEAD_DIM = 128
HEADS_DEV = 8
ROWS = 128
KV_GROUP = 2
DOCS = 8
TOPK = 8
NZ = 8
PLANE = 16
REACH = 5
CW = D // NZ
WCH = 4
WROWS = 512 // WCH
LOW = -1e30
COEF = math.log2(math.e) / math.sqrt(HEAD_DIM)
MESH = pl.DeviceIdType.MESH
OFFSET = (0, -1, -2, -3, 1, 2, 3, 4)
SCHEDULE = (
    "k1", "k2", "i1", "v0", "a0", "v1", "a1", "D0", "D1", "v2", "a2", "D2",
    "U0", "D3", "U1", "k3", "k4", "q0", "b0", "D4", "U2", "b1", "D5", "U3",
    "b2", "v3", "a3", "D6", "U4", "v4", "a4", "D7", "U5", "b3", "D8", "U6",
    "b4", "p0", "D9", "U7", "p4", "m0", "D10", "p1", "D11", "U8", "p5", "D12",
    "U9", "p2", "r0", "r4", "D13", "U10", "p6", "D14", "U11", "x0", "x4", "r1",
    "r5", "p3", "D15", "s0", "s4", "p7", "x1", "x5", "r2", "r6", "s1", "s5",
    "x2", "x6", "r3", "r7", "s2", "s6", "x3", "x7", "s3", "s7",
)


def kernel(
    q_ref, kv_ref, doc_ref, res_ref, w_ref, ids_ref, prio_ref,
    hid_out, rows_ref,
    hid_ref, qbuf, kvbuf, vt, mx, acc, att, wbuf, res, ids, prio, docs, mt, mtbuf, sel, psend, prec,
    xbuf, asend,
    in_s, kvu_s, kvu_r, kvy_s, kvy_r, q_s, q_r, w_s, w_r, ws_s, ws_r, mt_s, mt_r,
    p_s, p_r, x_s, x_r, y_s, y_r, a_s, a_r, l_s,
):
    ctx = lax.axis_index("ctx")
    head = lax.axis_index("head")
    core = lax.axis_index("dp")
    z = ctx // 2
    ylo = ctx % 2
    me = ylo * 8 + head

    def at_z(k):
        return {"ctx": ((z + k + NZ) % NZ) * 2 + ylo}

    def at_plane(p):
        return {"ctx": z * 2 + p // 8, "head": p % 8}

    partner = {"ctx": z * 2 + (1 - ylo)}
    sibling = {"dp": 1 - core}
    kind = head % 2
    twin = {"head": head + 1 - 2 * kind}

    def remote(src, dst, s, r, to):
        return pltpu.make_async_remote_copy(
            src_ref=src, dst_ref=dst, send_sem=s, recv_sem=r, device_id=to, device_id_type=MESH
        )

    def wait_for(ref, sem):
        pltpu.make_async_copy(ref, ref, sem).wait()

    key_head = pl.multiple_of((head // KV_GROUP) * HEAD_DIM, HEAD_DIM)
    loads = [
        pltpu.make_async_copy(src, dst, in_s.at[i])
        for i, (src, dst) in enumerate(
            (
                (kv_ref.at[:, :, pl.ds(key_head, HEAD_DIM)], kvbuf.at[0, :, 0]),
                (q_ref, qbuf.at[0]),
                (w_ref, wbuf.at[0]),
                (ids_ref, ids),
                (prio_ref, prio),
                (doc_ref, docs),
                (res_ref, res),
            )
        )
    ]
    for copy in loads:
        copy.start()

    barrier = pltpu.get_barrier_semaphore()

    def greet_plane(j, c):
        pl.semaphore_signal(barrier, inc=1, device_id=at_plane((me + j) % PLANE), device_id_type=MESH)
        return c

    def greet_z(j, c):
        pl.semaphore_signal(barrier, inc=1, device_id=at_z(j), device_id_type=MESH)
        return c

    lax.fori_loop(1, PLANE, greet_plane, 0)
    lax.fori_loop(1, NZ, greet_z, 0)
    pl.semaphore_signal(barrier, inc=1, device_id=sibling, device_id_type=MESH)

    def make_slots():
        row16 = lax.broadcasted_iota(jnp.int32, (16, 128), 0)
        lane16 = lax.broadcasted_iota(jnp.int32, (16, 128), 1)
        expert = lax.broadcasted_iota(jnp.int32, (128, 16), 0)
        chosen = jnp.zeros((128, 16), jnp.float32)
        for k in range(TOPK):
            chosen = chosen + jnp.where(ids[k : k + 1, :] == expert, 1.0, 0.0)
        prio_row = jnp.zeros((16, 128), jnp.int32)
        prio_col = jnp.zeros((16, 128), jnp.int32)
        for u in range(16):
            prio_row = jnp.where(lane16 == u, prio[u], prio_row)
            prio_col = jnp.where(row16 == u, prio[u], prio_col)
        earlier = jnp.where(prio_col < prio_row, 1.0, 0.0)[:, :16]
        ranks = jnp.dot(
            chosen.astype(jnp.bfloat16), earlier.astype(jnp.bfloat16), preferred_element_type=jnp.float32
        )
        slots = jnp.where(chosen > 0.5, ranks + 1.0, 0.0)
        place = jnp.where(lane16 == row16 + 16 * z, 1.0, 0.0)
        mt[...] = jnp.dot(
            slots.astype(jnp.bfloat16), place.astype(jnp.bfloat16), preferred_element_type=jnp.float32
        )

    pl.semaphore_wait(barrier, PLANE - 1 + NZ - 1 + 1)

    def kv_up(r):
        src = kvbuf.at[0 if r < 3 else 2, kind, 0]
        return remote(src, kvbuf.at[r, kind, 0], kvu_s.at[r], kvu_r.at[r], at_z(2 - r % 2))

    def kv_sides(r):
        if r == 0:
            return [remote(kvbuf.at[r, :, 0], kvbuf.at[r, :, 1], kvy_s.at[r, 0], kvy_r.at[r, 0], partner)]
        part = kvbuf.at[r, kind, 0]
        return [
            remote(part, kvbuf.at[r, kind, 1], kvy_s.at[r, 0], kvy_r.at[r, 0], partner),
            remote(part, kvbuf.at[r, kind, 1], kvy_s.at[r, 1], kvy_r.at[r, 1], partner | twin),
            remote(part, part, kvy_s.at[r, 2], kvy_r.at[r, 2], twin),
        ]

    def w_rows(c):
        return pl.ds(pl.multiple_of(core * 512 + c * WROWS, WROWS), WROWS)

    def w_ring(s, c):
        src = w_ref.at[w_rows(c), :] if s in (1, 4) else wbuf.at[s - 1, w_rows(c), :]
        to = at_z(1 if s < 4 else -1)
        return remote(src, wbuf.at[s, w_rows(c), :], w_s.at[s, c], w_r.at[s, c], to)

    def w_side(s, c):
        part = wbuf.at[s, w_rows(c), :]
        return remote(part, part, ws_s.at[s, c], ws_r.at[s, c], sibling)

    def w_forward(first, k):
        s, c = first + k // WCH, k % WCH
        w_ring(s, c).wait_recv()
        if s not in (3, 7):
            w_ring(s + 1, c).start()
        w_side(s, c).start()

    q_swap = remote(qbuf.at[0], qbuf.at[1], q_s, q_r, partner)
    for c in range(WCH):
        w_ring(4, c).start()
    loads[0].wait()
    kv_up(1).start()
    kv_sides(0)[0].start()
    kv_up(2).start()
    loads[1].wait()
    q_swap.start()
    for copy in loads[3:]:
        copy.wait()
    make_slots()

    def mt_copy(j):
        to = (z + j) % NZ
        rows = pl.ds(pl.multiple_of(to * 16, 16), 16)
        return remote(mt.at[rows, :], mtbuf.at[z], mt_s, mt_r, at_z(j))

    def mt_send(j, c):
        mt_copy(j).start()
        return c

    lax.fori_loop(1, NZ, mt_send, 0)
    mtbuf[z] = mt[pl.ds(pl.multiple_of(z * 16, 16), 16), :]

    row = lax.broadcasted_iota(jnp.int32, (2 * ROWS, ROWS), 0)
    lane = lax.broadcasted_iota(jnp.int32, (1, ROWS), 1)

    def attend(r, w):
        yq = ylo if w == 0 else 1 - ylo
        last = r == REACH - 1
        key_pos = ((z - r + NZ) % NZ) * 256 + (row + ylo * ROWS) % 256
        keys = kvbuf[r, 0].reshape(2 * ROWS, HEAD_DIM)
        if w == 0:
            vt[r, :HEAD_DIM, :] = kvbuf[r, 1].reshape(2 * ROWS, HEAD_DIM).T
            vt[r, HEAD_DIM:, :] = jnp.ones((16, 2 * ROWS), jnp.bfloat16)
        pos = (2 * z + yq) * ROWS + lane
        start = jnp.zeros((1, ROWS), jnp.int32)
        end = jnp.int32(0)
        for d in range(DOCS):
            length = docs[d]
            end = end + length
            start = start + jnp.where(pos >= end, length, 0)
        bias = jnp.where((key_pos <= pos) & (key_pos >= start), 0.0, LOW)
        bias = jnp.concatenate([bias, bias], axis=1)
        for pair in range(HEADS_DEV // 2):
            b = w * (HEADS_DEV // 2) + pair
            first = pair * 2 * HEAD_DIM
            query = jnp.concatenate(
                [
                    qbuf[w, :, first : first + HEAD_DIM],
                    qbuf[w, :, first + HEAD_DIM : first + 2 * HEAD_DIM],
                ],
                axis=0,
            )
            s = lax.dot_general(
                keys, query, (((1,), (1,)), ((), ())), preferred_element_type=jnp.float32
            )
            s = s + bias
            new = jnp.max(s, axis=0, keepdims=True)
            if r > 0:
                old = mx[b]
                new = jnp.maximum(old, new)
            weight = jnp.exp2((s - new) * COEF).astype(jnp.bfloat16)
            out = jnp.dot(vt[r], weight, preferred_element_type=jnp.float32)
            if r > 0:
                out = out + acc[b] * jnp.exp2((old - new) * COEF)
            if not last:
                mx[b] = new
                acc[b] = out
            else:
                mixed = out[:HEAD_DIM] / out[HEAD_DIM : HEAD_DIM + 1]
                for i in range(2):
                    one = mixed[:, i * ROWS : (i + 1) * ROWS].T.astype(jnp.bfloat16)
                    att[w, :, first + i * HEAD_DIM : first + (i + 1) * HEAD_DIM] = one

    def kv_step(r):
        kv_up(r).wait_recv()
        if r == 2:
            kv_up(3).start()
            kv_up(4).start()
        for copy in kv_sides(r):
            copy.start()

    def kv_wait(r):
        for copy in kv_sides(r):
            copy.wait_recv()

    def w_begin(s):
        for c in range(WCH):
            w_ring(s, c).start()

    def p_copy(o, w, h):
        to = (ylo if w == 0 else 1 - ylo) * 8 + h
        rows = pl.ds(pl.multiple_of(h * 16, 16), 16)
        return remote(psend.at[o, w, rows, :], prec.at[o, me], p_s.at[o], p_r.at[o], at_plane(to))

    def project(o, sides=(0, 1)):
        if 0 in sides:
            if o == 0:
                loads[2].wait()
            else:
                for c in range(WCH):
                    w_side(o, c).wait_recv()
        count = len(sides) * ROWS
        left = att[...].reshape(count, 1024) if count == 2 * ROWS else att[sides[0]]
        part = jnp.dot(left, wbuf[o], preferred_element_type=jnp.float32).astype(jnp.bfloat16)
        for i, w in enumerate(sides):
            psend[o, w] = part[i * ROWS : (i + 1) * ROWS]
            if w == 0:
                prec[o, me] = psend[o, 0, pl.ds(pl.multiple_of(head * 16, 16), 16), :]

            def send(j, c, w=w):
                p_copy(o, w, (head + j) % 8).start()
                return c

            lax.fori_loop(1 - w, 8, send, 0)

    def make_selection():
        row16 = lax.broadcasted_iota(jnp.int32, (16, 128), 0)
        lane16 = lax.broadcasted_iota(jnp.int32, (16, 128), 1)
        wait_for(mtbuf.at[pl.ds(0, NZ - 1)], mt_r)
        table = mtbuf[0]
        for i in range(1, NZ):
            table = table + mtbuf[i]
        want = jnp.where(lane16 // 16 == row16 // 2, (row16 % 2 + 1).astype(jnp.float32), -1.0)
        for d in range(PLANE):
            hit = jnp.broadcast_to(table[d : d + 1, :], (16, 128)) == want
            sel[pl.ds(d * 16, 16), :] = jnp.where(hit, 1.0, 0.0).astype(jnp.bfloat16)

    def x_copy(o, k, far):
        part = xbuf.at[(z + k + NZ) % NZ, :, pl.ds(o * CW, CW)]
        if k == 0 and far in (2, -2):
            way = 0 if far > 0 else 1
            return remote(part, part, y_s.at[o, way], y_r.at[o, way], at_z(far))
        return remote(part, part, x_s.at[o], x_r.at[o], at_z(far))

    def x_passed(o):
        return ((-2, 1), (2, -1), (-2, 2) if o % 2 else (2, -2))

    def x_forward(o):
        x_copy(o, 0, 2).wait_recv()
        x_copy(o, 0, -2).wait_recv()
        for k, far in x_passed(o):
            x_copy(o, k, far).start()

    def reduce(o):
        wait_for(prec.at[o, pl.ds(0, PLANE - 1)], p_r.at[o])
        halves = []
        for side in range(2):
            total = jnp.zeros((16, 256), jnp.float32)
            for h in range(8):
                total = total + prec[o, side * 8 + h].astype(jnp.float32)
            halves.append(total)
        total = jnp.concatenate(halves, axis=1)
        cols = pl.ds(pl.multiple_of(((z + OFFSET[o] + NZ) % NZ) * CW, CW), CW)
        hidden = (res[:, cols].astype(jnp.float32) + total).astype(jnp.bfloat16)
        hid_ref[:, cols] = hidden
        xbuf[z, :, o * CW : (o + 1) * CW] = hidden

        for far in (2, -2, 1, -1):
            x_copy(o, 0, far).start()

    def a_copy(o, j):
        to = (me + j) % PLANE
        cols = pl.ds(o * CW, CW)
        return remote(asend.at[to, :, cols], rows_ref.at[me, :, cols], a_s.at[o], a_r.at[o], at_plane(to))

    def own_copy(o):
        cols = pl.ds(o * CW, CW)
        return pltpu.make_async_copy(asend.at[me, :, cols], rows_ref.at[me, :, cols], l_s.at[o])

    def select(o):
        wait_for(xbuf.at[pl.ds(0, 5), :, pl.ds(o * CW, CW)], x_r.at[o])
        cols = slice(o * CW, (o + 1) * CW)
        gathered = xbuf[:, :, cols].reshape(ROWS, CW)
        picked = jnp.dot(sel[...], gathered, preferred_element_type=jnp.float32)
        asend[:, :, cols] = picked.astype(jnp.bfloat16).reshape(PLANE, 16, CW)

        def send(j, c):
            a_copy(o, j).start()
            return c

        lax.fori_loop(1, PLANE, send, 0)
        own_copy(o).start()

    hid_copy = pltpu.make_async_copy(hid_ref, hid_out, l_s.at[NZ])

    steps = {
        "a": lambda r: attend(r, 0),
        "b": lambda r: attend(r, 1),
        "k": kv_step,
        "v": kv_wait,
        "q": lambda r: q_swap.wait_recv(),
        "i": w_begin,
        "D": lambda k: w_forward(4, k),
        "U": lambda k: w_forward(1, k),
        "p": project,
        "P": lambda o: project(o, (0,)),
        "Q": lambda o: project(o, (1,)),
        "m": lambda r: make_selection(),
        "r": reduce,
        "x": x_forward,
        "s": select,
    }
    for step in SCHEDULE:
        steps[step[0]](int(step[1:]))
    hid_copy.start()

    hid_copy.wait()
    for r in range(1, REACH):
        kv_up(r).wait_send()
    for r in range(REACH):
        for copy in kv_sides(r):
            copy.wait_send()
    q_swap.wait_send()
    for s in range(1, NZ):
        for c in range(WCH):
            w_ring(s, c).wait_send()
            w_side(s, c).wait_send()
    wait_for(mtbuf.at[pl.ds(0, NZ - 1)], mt_s)
    for o in range(NZ):
        wait_for(prec.at[o, pl.ds(0, PLANE - 1)], p_s.at[o])
        wait_for(xbuf.at[pl.ds(0, 5), :, pl.ds(o * CW, CW)], x_s.at[o])
        for far in (2, -2):
            x_copy(o, 0, far).wait_send()
        wait_for(asend.at[pl.ds(0, PLANE - 1), :, pl.ds(o * CW, CW)], a_s.at[o])
        own_copy(o).wait()
    for o in range(NZ):
        wait_for(asend.at[pl.ds(0, PLANE - 1), :, pl.ds(o * CW, CW)], a_r.at[o])


def finish(
    hid_ref, rows_ref, gain_ref, hid_out, rows_out, hid, rows, gain, wide_gain, out, sem
):
    ins = [pltpu.make_async_copy(gain_ref, gain, sem.at[0, 0]), pltpu.make_async_copy(hid_ref, hid, sem.at[0, 1])]
    for copy in ins:
        copy.start()
    to_hid = pltpu.make_async_copy(hid, hid_out, sem.at[1, 0])

    def row_in(p):
        return pltpu.make_async_copy(rows_ref.at[p], rows.at[p], sem.at[2, p])

    def row_out(p):
        return pltpu.make_async_copy(out.at[:, p], rows_out.at[:, p], sem.at[3, p])

    def begin(p, c):
        row_in(p).start()
        return c

    lax.fori_loop(0, PLANE, begin, 0)
    ins[0].wait()
    for k in range(NZ):
        for o in range(NZ):
            first = ((k + OFFSET[o]) % NZ) * CW
            part = jnp.broadcast_to(gain[:, first : first + CW], (2, CW))
            wide_gain[2 * k : 2 * k + 2, o * CW : (o + 1) * CW] = part
    ins[1].wait()
    to_hid.start()

    def one(p, c):
        row_in(p).wait()
        squares = jnp.zeros((16, CW), jnp.float32)
        for o in range(NZ):
            value = rows[p, :, o * CW : (o + 1) * CW].astype(jnp.float32)
            squares = squares + value * value
        scale = lax.rsqrt(jnp.sum(squares, axis=1, keepdims=True) / D + 1e-06)
        for o in range(NZ):
            cols = slice(o * CW, (o + 1) * CW)
            value = rows[p, :, cols].astype(jnp.float32) * scale * wide_gain[:, cols]
            value = value.astype(jnp.bfloat16).reshape(NZ, 2, CW)
            for k in range(NZ):
                first = ((k + OFFSET[o]) % NZ) * CW
                out[k, p, :, first : first + CW] = value[k]
        row_out(p).start()
        return c

    lax.fori_loop(0, PLANE, one, 0)

    def end(p, c):
        row_out(p).wait()
        return c

    lax.fori_loop(0, PLANE, end, 0)
    to_hid.wait()


def local(queries, keys_values, doc_lengths, residual, out_weight, norm_gain, expert_ids, priority):
    anywhere = pl.BlockSpec(memory_space=pl.ANY)
    bf16, f32 = jnp.bfloat16, jnp.float32
    dma = pltpu.SemaphoreType.DMA
    wide_gain = norm_gain.reshape(1, D)
    hidden, rows = pl.pallas_call(
        kernel,
        out_shape=(
            jax.ShapeDtypeStruct((16, D), bf16),
            jax.ShapeDtypeStruct((PLANE, 16, D), bf16),
        ),
        in_specs=[anywhere] * 7,
        out_specs=(anywhere, anywhere),
        scratch_shapes=[
            pltpu.VMEM((16, D), bf16),
            pltpu.VMEM((2, ROWS, 1024), bf16),
            pltpu.VMEM((REACH, 2, 2, ROWS, HEAD_DIM), bf16),
            pltpu.VMEM((REACH, HEAD_DIM + 16, 2 * ROWS), bf16),
            pltpu.VMEM((HEADS_DEV, 1, 2 * ROWS), f32),
            pltpu.VMEM((HEADS_DEV, HEAD_DIM + 16, 2 * ROWS), f32),
            pltpu.VMEM((2, ROWS, 1024), bf16),
            pltpu.VMEM((NZ, 1024, 256), bf16),
            pltpu.VMEM((16, D), bf16),
            pltpu.VMEM((TOPK, 16), jnp.int32),
            pltpu.SMEM((16,), jnp.int32),
            pltpu.SMEM((DOCS,), jnp.int32),
            pltpu.VMEM((128, 128), f32),
            pltpu.VMEM((NZ, 16, 128), f32),
            pltpu.VMEM((256, 128), bf16),
            pltpu.VMEM((NZ, 2, ROWS, 256), bf16),
            pltpu.VMEM((NZ, PLANE, 16, 256), bf16),
            pltpu.VMEM((NZ, 16, D), bf16),
            pltpu.VMEM((PLANE, 16, D), bf16),
            dma((7,)),
            dma((REACH,)), dma((REACH,)), dma((REACH, 3)), dma((REACH, 3)),
            dma(()), dma(()),
            dma((NZ, WCH)), dma((NZ, WCH)), dma((NZ, WCH)), dma((NZ, WCH)),
            dma(()), dma(()),
            dma((NZ,)), dma((NZ,)),
            dma((NZ,)), dma((NZ,)), dma((NZ, 2)), dma((NZ, 2)),
            dma((NZ,)), dma((NZ,)), dma((NZ + 1,)),
        ],
        compiler_params=pltpu.CompilerParams(
            collective_id=0, has_side_effects=True, vmem_limit_bytes=62 * 1024 * 1024
        ),
    )(
        queries, keys_values, doc_lengths, residual, out_weight,
        expert_ids.T, priority,
    )
    hidden, rows = pl.pallas_call(
        finish,
        out_shape=(
            jax.ShapeDtypeStruct((16, D), bf16),
            jax.ShapeDtypeStruct((NZ, PLANE, 2, D), bf16),
        ),
        in_specs=[anywhere] * 3,
        out_specs=(anywhere, anywhere),
        scratch_shapes=[
            pltpu.VMEM((16, D), bf16),
            pltpu.VMEM((PLANE, 16, D), bf16),
            pltpu.VMEM((1, D), f32),
            pltpu.VMEM((16, D), f32),
            pltpu.VMEM((NZ, PLANE, 2, D), bf16),
            dma((4, PLANE)),
        ],
        compiler_params=pltpu.CompilerParams(vmem_limit_bytes=62 * 1024 * 1024),
    )(hidden, rows, wide_gain)
    return hidden, rows.reshape(1, PLANE * NZ, 2, D)


def solution(mesh):
    return jax.shard_map(
        local,
        mesh=mesh,
        in_specs=(
            P(("dp", "ctx"), "head"),
            P(None, ("dp", "ctx"), None),
            P("dp"),
            P(("dp", "ctx", "head"), None),
            P("head", "ctx"),
            P(),
            P(("dp", "ctx", "head"), None),
            P(("dp", "ctx", "head")),
        ),
        out_specs=(P(("dp", "ctx", "head"), None), P(("ctx", "head"), "dp", None, None)),
        check_vma=False,
    )
```

```python
import math

import jax
import jax.numpy as jnp
from jax import lax
from jax.experimental import pallas as pl
from jax.experimental.pallas import tpu as pltpu
from jax.sharding import PartitionSpec as P

D = 4096
HEAD_DIM = 128
HEADS_DEV = 8
ROWS = 128
KV_GROUP = 2
DOCS = 8
TOPK = 8
NZ = 8
PLANE = 16
REACH = 5
CW = D // NZ
WCH = 4
WROWS = 512 // WCH
LOW = -1e30
COEF = math.log2(math.e) / math.sqrt(HEAD_DIM)
MESH = pl.DeviceIdType.MESH
OFFSET = (0, -1, -2, -3, 1, 2, 3, 4)
SCHEDULE = (
    "k1", "i1", "k2", "D0", "v0", "a0", "D1", "v1", "a1", "D2", "v2", "a2",
    "D3", "U0", "k3", "k4", "D4", "U1", "q0", "b0", "D5", "U2", "b1", "D6",
    "U3", "v3", "a3", "D7", "U4", "v4", "a4", "D8", "U5", "b2", "D9", "U6",
    "b3", "D10", "U7", "b4", "p0", "D11", "U8", "p4", "m0", "D12", "U9", "p1",
    "D13", "U10", "p5", "U11", "p2", "r0", "r4", "U12", "U13", "p6", "r1", "r5",
    "x0", "x4", "p3", "p7", "x1", "x5", "s0", "s4", "r2", "r6", "s1", "x2",
    "r3", "s5", "x6", "r7", "s2", "x3", "s6", "x7", "s3", "s7",
)


def kernel(
    q_ref, kv_ref, doc_ref, res_ref, w_ref, ids_ref, prio_ref,
    hid_out, rows_ref,
    hid_ref, qbuf, kvbuf, vt, mx, acc, att, wbuf, res, ids, prio, docs, mt, mtbuf, sel, psend, prec,
    xbuf, asend,
    in_s, kvu_s, kvu_r, kvy_s, kvy_r, q_s, q_r, w_s, w_r, ws_s, ws_r, mt_s, mt_r,
    p_s, p_r, x_s, x_r, y_s, y_r, a_s, a_r, l_s,
):
    ctx = lax.axis_index("ctx")
    head = lax.axis_index("head")
    core = lax.axis_index("dp")
    z = ctx // 2
    ylo = ctx % 2
    me = ylo * 8 + head

    def at_z(k):
        return {"ctx": ((z + k + NZ) % NZ) * 2 + ylo}

    def at_plane(p):
        return {"ctx": z * 2 + p // 8, "head": p % 8}

    partner = {"ctx": z * 2 + (1 - ylo)}
    sibling = {"dp": 1 - core}
    kind = head % 2
    twin = {"head": head + 1 - 2 * kind}

    def remote(src, dst, s, r, to):
        return pltpu.make_async_remote_copy(
            src_ref=src, dst_ref=dst, send_sem=s, recv_sem=r, device_id=to, device_id_type=MESH
        )

    def wait_for(ref, sem):
        pltpu.make_async_copy(ref, ref, sem).wait()

    key_head = pl.multiple_of((head // KV_GROUP) * HEAD_DIM, HEAD_DIM)
    loads = [
        pltpu.make_async_copy(src, dst, in_s.at[i])
        for i, (src, dst) in enumerate(
            (
                (kv_ref.at[:, :, pl.ds(key_head, HEAD_DIM)], kvbuf.at[0, :, 0]),
                (q_ref, qbuf.at[0]),
                (w_ref, wbuf.at[0]),
                (ids_ref, ids),
                (prio_ref, prio),
                (doc_ref, docs),
                (res_ref, res),
            )
        )
    ]
    for copy in loads:
        copy.start()

    barrier = pltpu.get_barrier_semaphore()

    def greet_plane(j, c):
        pl.semaphore_signal(barrier, inc=1, device_id=at_plane((me + j) % PLANE), device_id_type=MESH)
        return c

    def greet_z(j, c):
        pl.semaphore_signal(barrier, inc=1, device_id=at_z(j), device_id_type=MESH)
        return c

    lax.fori_loop(1, PLANE, greet_plane, 0)
    lax.fori_loop(1, NZ, greet_z, 0)
    pl.semaphore_signal(barrier, inc=1, device_id=sibling, device_id_type=MESH)

    def make_slots():
        row16 = lax.broadcasted_iota(jnp.int32, (16, 128), 0)
        lane16 = lax.broadcasted_iota(jnp.int32, (16, 128), 1)
        expert = lax.broadcasted_iota(jnp.int32, (128, 16), 0)
        chosen = jnp.zeros((128, 16), jnp.float32)
        for k in range(TOPK):
            chosen = chosen + jnp.where(ids[k : k + 1, :] == expert, 1.0, 0.0)
        prio_row = jnp.zeros((16, 128), jnp.int32)
        prio_col = jnp.zeros((16, 128), jnp.int32)
        for u in range(16):
            prio_row = jnp.where(lane16 == u, prio[u], prio_row)
            prio_col = jnp.where(row16 == u, prio[u], prio_col)
        earlier = jnp.where(prio_col < prio_row, 1.0, 0.0)[:, :16]
        ranks = jnp.dot(
            chosen.astype(jnp.bfloat16), earlier.astype(jnp.bfloat16), preferred_element_type=jnp.float32
        )
        slots = jnp.where(chosen > 0.5, ranks + 1.0, 0.0)
        place = jnp.where(lane16 == row16 + 16 * z, 1.0, 0.0)
        mt[...] = jnp.dot(
            slots.astype(jnp.bfloat16), place.astype(jnp.bfloat16), preferred_element_type=jnp.float32
        )

    pl.semaphore_wait(barrier, PLANE - 1 + NZ - 1 + 1)

    def kv_up(r):
        src = kvbuf.at[0 if r < 3 else 2, kind, 0]
        return remote(src, kvbuf.at[r, kind, 0], kvu_s.at[r], kvu_r.at[r], at_z(2 - r % 2))

    def kv_sides(r):
        if r == 0:
            return [remote(kvbuf.at[r, :, 0], kvbuf.at[r, :, 1], kvy_s.at[r, 0], kvy_r.at[r, 0], partner)]
        part = kvbuf.at[r, kind, 0]
        return [
            remote(part, kvbuf.at[r, kind, 1], kvy_s.at[r, 0], kvy_r.at[r, 0], partner),
            remote(part, kvbuf.at[r, kind, 1], kvy_s.at[r, 1], kvy_r.at[r, 1], partner | twin),
            remote(part, part, kvy_s.at[r, 2], kvy_r.at[r, 2], twin),
        ]

    def w_rows(c):
        return pl.ds(pl.multiple_of(core * 512 + c * WROWS, WROWS), WROWS)

    def w_ring(s, c):
        up = s < 4 or (s == 7 and c >= WCH // 2)
        before = 3 if s == 7 and up else s - 1
        src = w_ref.at[w_rows(c), :] if s in (1, 4) else wbuf.at[before, w_rows(c), :]
        to = at_z(1 if up else -1)
        return remote(src, wbuf.at[s, w_rows(c), :], w_s.at[s, c], w_r.at[s, c], to)

    def w_side(s, c):
        part = wbuf.at[s, w_rows(c), :]
        return remote(part, part, ws_s.at[s, c], ws_r.at[s, c], sibling)

    def w_forward(first, k):
        s, c = first + k // WCH, k % WCH
        if first == 1 and s == 4:
            s, c = 7, c + WCH // 2
        w_ring(s, c).wait_recv()
        if s == 3 and c >= WCH // 2 or s == 6 and c < WCH // 2:
            w_ring(7, c).start()
        elif s not in (3, 6, 7):
            w_ring(s + 1, c).start()
        w_side(s, c).start()

    q_swap = remote(qbuf.at[0], qbuf.at[1], q_s, q_r, partner)
    for c in range(WCH):
        w_ring(4, c).start()
    loads[0].wait()
    kv_up(1).start()
    kv_sides(0)[0].start()
    kv_up(2).start()
    loads[1].wait()
    q_swap.start()
    for copy in loads[3:]:
        copy.wait()
    make_slots()

    def mt_copy(j):
        to = (z + j) % NZ
        rows = pl.ds(pl.multiple_of(to * 16, 16), 16)
        return remote(mt.at[rows, :], mtbuf.at[z], mt_s, mt_r, at_z(j))

    def mt_send(j, c):
        mt_copy(j).start()
        return c

    lax.fori_loop(1, NZ, mt_send, 0)
    mtbuf[z] = mt[pl.ds(pl.multiple_of(z * 16, 16), 16), :]

    row = lax.broadcasted_iota(jnp.int32, (2 * ROWS, ROWS), 0)
    lane = lax.broadcasted_iota(jnp.int32, (1, ROWS), 1)

    def attend(r, w):
        yq = ylo if w == 0 else 1 - ylo
        last = r == REACH - 1
        key_pos = ((z - r + NZ) % NZ) * 256 + (row + ylo * ROWS) % 256
        keys = kvbuf[r, 0].reshape(2 * ROWS, HEAD_DIM)
        if w == 0:
            vt[r, :HEAD_DIM, :] = kvbuf[r, 1].reshape(2 * ROWS, HEAD_DIM).T
            vt[r, HEAD_DIM:, :] = jnp.ones((16, 2 * ROWS), jnp.bfloat16)
        pos = (2 * z + yq) * ROWS + lane
        start = jnp.zeros((1, ROWS), jnp.int32)
        end = jnp.int32(0)
        for d in range(DOCS):
            length = docs[d]
            end = end + length
            start = start + jnp.where(pos >= end, length, 0)
        bias = jnp.where((key_pos <= pos) & (key_pos >= start), 0.0, LOW)
        bias = jnp.concatenate([bias, bias], axis=1)
        for pair in range(HEADS_DEV // 2):
            b = w * (HEADS_DEV // 2) + pair
            first = pair * 2 * HEAD_DIM
            query = jnp.concatenate(
                [
                    qbuf[w, :, first : first + HEAD_DIM],
                    qbuf[w, :, first + HEAD_DIM : first + 2 * HEAD_DIM],
                ],
                axis=0,
            )
            s = lax.dot_general(
                keys, query, (((1,), (1,)), ((), ())), preferred_element_type=jnp.float32
            )
            s = s + bias
            new = jnp.max(s, axis=0, keepdims=True)
            if r > 0:
                old = mx[b]
                new = jnp.maximum(old, new)
            weight = jnp.exp2((s - new) * COEF).astype(jnp.bfloat16)
            out = jnp.dot(vt[r], weight, preferred_element_type=jnp.float32)
            if r > 0:
                out = out + acc[b] * jnp.exp2((old - new) * COEF)
            if not last:
                mx[b] = new
                acc[b] = out
            else:
                mixed = out[:HEAD_DIM] / out[HEAD_DIM : HEAD_DIM + 1]
                for i in range(2):
                    one = mixed[:, i * ROWS : (i + 1) * ROWS].T.astype(jnp.bfloat16)
                    att[w, :, first + i * HEAD_DIM : first + (i + 1) * HEAD_DIM] = one

    def kv_step(r):
        kv_up(r).wait_recv()
        if r == 2:
            kv_up(3).start()
            kv_up(4).start()
        for copy in kv_sides(r):
            copy.start()

    def kv_wait(r):
        for copy in kv_sides(r):
            copy.wait_recv()

    def w_begin(s):
        for c in range(WCH):
            w_ring(s, c).start()

    def p_copy(o, w, h):
        to = (ylo if w == 0 else 1 - ylo) * 8 + h
        rows = pl.ds(pl.multiple_of(h * 16, 16), 16)
        return remote(psend.at[o, w, rows, :], prec.at[o, me], p_s.at[o], p_r.at[o], at_plane(to))

    def project(o, sides=(0, 1)):
        if 0 in sides:
            if o == 0:
                loads[2].wait()
            else:
                for c in range(WCH):
                    w_side(o, c).wait_recv()
        count = len(sides) * ROWS
        left = att[...].reshape(count, 1024) if count == 2 * ROWS else att[sides[0]]
        part = jnp.dot(left, wbuf[o], preferred_element_type=jnp.float32).astype(jnp.bfloat16)
        for i, w in enumerate(sides):
            psend[o, w] = part[i * ROWS : (i + 1) * ROWS]
            if w == 0:
                prec[o, me] = psend[o, 0, pl.ds(pl.multiple_of(head * 16, 16), 16), :]

            def send(j, c, w=w):
                p_copy(o, w, (head + j) % 8).start()
                return c

            lax.fori_loop(1 - w, 8, send, 0)

    def make_selection():
        row16 = lax.broadcasted_iota(jnp.int32, (16, 128), 0)
        lane16 = lax.broadcasted_iota(jnp.int32, (16, 128), 1)
        wait_for(mtbuf.at[pl.ds(0, NZ - 1)], mt_r)
        table = mtbuf[0]
        for i in range(1, NZ):
            table = table + mtbuf[i]
        want = jnp.where(lane16 // 16 == row16 // 2, (row16 % 2 + 1).astype(jnp.float32), -1.0)
        for d in range(PLANE):
            hit = jnp.broadcast_to(table[d : d + 1, :], (16, 128)) == want
            sel[pl.ds(d * 16, 16), :] = jnp.where(hit, 1.0, 0.0).astype(jnp.bfloat16)

    def x_copy(o, k, far):
        part = xbuf.at[(z + k + NZ) % NZ, :, pl.ds(o * CW, CW)]
        if k == 0 and far in (2, -2):
            way = 0 if far > 0 else 1
            return remote(part, part, y_s.at[o, way], y_r.at[o, way], at_z(far))
        return remote(part, part, x_s.at[o], x_r.at[o], at_z(far))

    def x_passed(o):
        return ((-2, 1), (2, -1), (-2, 2) if o % 2 else (2, -2))

    def x_forward(o):
        x_copy(o, 0, 2).wait_recv()
        x_copy(o, 0, -2).wait_recv()
        for k, far in x_passed(o):
            x_copy(o, k, far).start()

    def reduce(o):
        wait_for(prec.at[o, pl.ds(0, PLANE - 1)], p_r.at[o])
        halves = []
        for side in range(2):
            total = jnp.zeros((16, 256), jnp.float32)
            for h in range(8):
                total = total + prec[o, side * 8 + h].astype(jnp.float32)
            halves.append(total)
        total = jnp.concatenate(halves, axis=1)
        cols = pl.ds(pl.multiple_of(((z + OFFSET[o] + NZ) % NZ) * CW, CW), CW)
        hidden = (res[:, cols].astype(jnp.float32) + total).astype(jnp.bfloat16)
        hid_ref[:, cols] = hidden
        xbuf[z, :, o * CW : (o + 1) * CW] = hidden

        for far in (2, -2, 1, -1):
            x_copy(o, 0, far).start()

    def a_copy(o, j):
        to = (me + j) % PLANE
        cols = pl.ds(o * CW, CW)
        return remote(asend.at[to, :, cols], rows_ref.at[me, :, cols], a_s.at[o], a_r.at[o], at_plane(to))

    def own_copy(o):
        cols = pl.ds(o * CW, CW)
        return pltpu.make_async_copy(asend.at[me, :, cols], rows_ref.at[me, :, cols], l_s.at[o])

    def select(o):
        wait_for(xbuf.at[pl.ds(0, 5), :, pl.ds(o * CW, CW)], x_r.at[o])
        cols = slice(o * CW, (o + 1) * CW)
        gathered = xbuf[:, :, cols].reshape(ROWS, CW)
        picked = jnp.dot(sel[...], gathered, preferred_element_type=jnp.float32)
        asend[:, :, cols] = picked.astype(jnp.bfloat16).reshape(PLANE, 16, CW)

        def send(j, c):
            a_copy(o, j).start()
            return c

        lax.fori_loop(1, PLANE, send, 0)
        own_copy(o).start()

    hid_copy = pltpu.make_async_copy(hid_ref, hid_out, l_s.at[NZ])

    steps = {
        "a": lambda r: attend(r, 0),
        "b": lambda r: attend(r, 1),
        "k": kv_step,
        "v": kv_wait,
        "q": lambda r: q_swap.wait_recv(),
        "i": w_begin,
        "D": lambda k: w_forward(4, k),
        "U": lambda k: w_forward(1, k),
        "p": project,
        "P": lambda o: project(o, (0,)),
        "Q": lambda o: project(o, (1,)),
        "m": lambda r: make_selection(),
        "r": reduce,
        "x": x_forward,
        "s": select,
    }
    for step in SCHEDULE:
        steps[step[0]](int(step[1:]))
    hid_copy.start()

    hid_copy.wait()
    for r in range(1, REACH):
        kv_up(r).wait_send()
    for r in range(REACH):
        for copy in kv_sides(r):
            copy.wait_send()
    q_swap.wait_send()
    for s in range(1, NZ):
        for c in range(WCH):
            w_ring(s, c).wait_send()
            w_side(s, c).wait_send()
    wait_for(mtbuf.at[pl.ds(0, NZ - 1)], mt_s)
    for o in range(NZ):
        wait_for(prec.at[o, pl.ds(0, PLANE - 1)], p_s.at[o])
        wait_for(xbuf.at[pl.ds(0, 5), :, pl.ds(o * CW, CW)], x_s.at[o])
        for far in (2, -2):
            x_copy(o, 0, far).wait_send()
        wait_for(asend.at[pl.ds(0, PLANE - 1), :, pl.ds(o * CW, CW)], a_s.at[o])
        own_copy(o).wait()
    for o in range(NZ):
        wait_for(asend.at[pl.ds(0, PLANE - 1), :, pl.ds(o * CW, CW)], a_r.at[o])


def finish(
    hid_ref, rows_ref, gain_ref, hid_out, rows_out, hid, rows, gain, wide_gain, out, sem
):
    ins = [pltpu.make_async_copy(gain_ref, gain, sem.at[0, 0]), pltpu.make_async_copy(hid_ref, hid, sem.at[0, 1])]
    for copy in ins:
        copy.start()
    to_hid = pltpu.make_async_copy(hid, hid_out, sem.at[1, 0])

    def row_in(p):
        return pltpu.make_async_copy(rows_ref.at[p], rows.at[p], sem.at[2, p])

    def row_out(p):
        return pltpu.make_async_copy(out.at[:, p], rows_out.at[:, p], sem.at[3, p])

    def begin(p, c):
        row_in(p).start()
        return c

    lax.fori_loop(0, PLANE, begin, 0)
    ins[0].wait()
    for k in range(NZ):
        for o in range(NZ):
            first = ((k + OFFSET[o]) % NZ) * CW
            part = jnp.broadcast_to(gain[:, first : first + CW], (2, CW))
            wide_gain[2 * k : 2 * k + 2, o * CW : (o + 1) * CW] = part
    ins[1].wait()
    to_hid.start()

    def one(p, c):
        row_in(p).wait()
        squares = jnp.zeros((16, CW), jnp.float32)
        for o in range(NZ):
            value = rows[p, :, o * CW : (o + 1) * CW].astype(jnp.float32)
            squares = squares + value * value
        scale = lax.rsqrt(jnp.sum(squares, axis=1, keepdims=True) / D + 1e-06)
        for o in range(NZ):
            cols = slice(o * CW, (o + 1) * CW)
            value = rows[p, :, cols].astype(jnp.float32) * scale * wide_gain[:, cols]
            value = value.astype(jnp.bfloat16).reshape(NZ, 2, CW)
            for k in range(NZ):
                first = ((k + OFFSET[o]) % NZ) * CW
                out[k, p, :, first : first + CW] = value[k]
        row_out(p).start()
        return c

    lax.fori_loop(0, PLANE, one, 0)

    def end(p, c):
        row_out(p).wait()
        return c

    lax.fori_loop(0, PLANE, end, 0)
    to_hid.wait()


def local(queries, keys_values, doc_lengths, residual, out_weight, norm_gain, expert_ids, priority):
    anywhere = pl.BlockSpec(memory_space=pl.ANY)
    bf16, f32 = jnp.bfloat16, jnp.float32
    dma = pltpu.SemaphoreType.DMA
    wide_gain = norm_gain.reshape(1, D)
    hidden, rows = pl.pallas_call(
        kernel,
        out_shape=(
            jax.ShapeDtypeStruct((16, D), bf16),
            jax.ShapeDtypeStruct((PLANE, 16, D), bf16),
        ),
        in_specs=[anywhere] * 7,
        out_specs=(anywhere, anywhere),
        scratch_shapes=[
            pltpu.VMEM((16, D), bf16),
            pltpu.VMEM((2, ROWS, 1024), bf16),
            pltpu.VMEM((REACH, 2, 2, ROWS, HEAD_DIM), bf16),
            pltpu.VMEM((REACH, HEAD_DIM + 16, 2 * ROWS), bf16),
            pltpu.VMEM((HEADS_DEV, 1, 2 * ROWS), f32),
            pltpu.VMEM((HEADS_DEV, HEAD_DIM + 16, 2 * ROWS), f32),
            pltpu.VMEM((2, ROWS, 1024), bf16),
            pltpu.VMEM((NZ, 1024, 256), bf16),
            pltpu.VMEM((16, D), bf16),
            pltpu.VMEM((TOPK, 16), jnp.int32),
            pltpu.SMEM((16,), jnp.int32),
            pltpu.SMEM((DOCS,), jnp.int32),
            pltpu.VMEM((128, 128), f32),
            pltpu.VMEM((NZ, 16, 128), f32),
            pltpu.VMEM((256, 128), bf16),
            pltpu.VMEM((NZ, 2, ROWS, 256), bf16),
            pltpu.VMEM((NZ, PLANE, 16, 256), bf16),
            pltpu.VMEM((NZ, 16, D), bf16),
            pltpu.VMEM((PLANE, 16, D), bf16),
            dma((7,)),
            dma((REACH,)), dma((REACH,)), dma((REACH, 3)), dma((REACH, 3)),
            dma(()), dma(()),
            dma((NZ, WCH)), dma((NZ, WCH)), dma((NZ, WCH)), dma((NZ, WCH)),
            dma(()), dma(()),
            dma((NZ,)), dma((NZ,)),
            dma((NZ,)), dma((NZ,)), dma((NZ, 2)), dma((NZ, 2)),
            dma((NZ,)), dma((NZ,)), dma((NZ + 1,)),
        ],
        compiler_params=pltpu.CompilerParams(
            collective_id=0, has_side_effects=True, vmem_limit_bytes=62 * 1024 * 1024
        ),
    )(
        queries, keys_values, doc_lengths, residual, out_weight,
        expert_ids.T, priority,
    )
    hidden, rows = pl.pallas_call(
        finish,
        out_shape=(
            jax.ShapeDtypeStruct((16, D), bf16),
            jax.ShapeDtypeStruct((NZ, PLANE, 2, D), bf16),
        ),
        in_specs=[anywhere] * 3,
        out_specs=(anywhere, anywhere),
        scratch_shapes=[
            pltpu.VMEM((16, D), bf16),
            pltpu.VMEM((PLANE, 16, D), bf16),
            pltpu.VMEM((1, D), f32),
            pltpu.VMEM((16, D), f32),
            pltpu.VMEM((NZ, PLANE, 2, D), bf16),
            dma((4, PLANE)),
        ],
        compiler_params=pltpu.CompilerParams(vmem_limit_bytes=62 * 1024 * 1024),
    )(hidden, rows, wide_gain)
    return hidden, rows.reshape(1, PLANE * NZ, 2, D)


def solution(mesh):
    return jax.shard_map(
        local,
        mesh=mesh,
        in_specs=(
            P(("dp", "ctx"), "head"),
            P(None, ("dp", "ctx"), None),
            P("dp"),
            P(("dp", "ctx", "head"), None),
            P("head", "ctx"),
            P(),
            P(("dp", "ctx", "head"), None),
            P(("dp", "ctx", "head")),
        ),
        out_specs=(P(("dp", "ctx", "head"), None), P(("ctx", "head"), "dp", None, None)),
        check_vma=False,
    )
```

```python
import math

import jax
import jax.numpy as jnp
from jax import lax
from jax.experimental import pallas as pl
from jax.experimental.pallas import tpu as pltpu
from jax.sharding import PartitionSpec as P

D = 4096
HEAD_DIM = 128
HEADS_DEV = 8
ROWS = 128
KV_GROUP = 2
DOCS = 8
TOPK = 8
NZ = 8
PLANE = 16
REACH = 5
CW = D // NZ
WCH = 4
WROWS = 512 // WCH
LOW = -1e30
COEF = math.log2(math.e) / math.sqrt(HEAD_DIM)
MESH = pl.DeviceIdType.MESH
OFFSET = (0, -1, -2, -3, 1, 2, 3, 4)
SCHEDULE = (
    "k1", "i1", "k2", "D0", "v0", "a0", "D1", "v1", "a1", "D2", "v2", "a2",
    "D3", "U0", "k3", "k4", "D4", "U1", "q0", "b0", "D5", "U2", "b1", "D6",
    "U3", "v3", "a3", "D7", "U4", "v4", "a4", "D8", "U5", "b2", "D9", "U6",
    "b3", "D10", "U7", "b4", "p0", "D11", "U8", "p4", "m0", "D12", "U9", "p1",
    "D13", "U10", "p5", "U11", "p2", "r0", "r4", "U12", "U13", "p6", "r1", "r5",
    "x0", "x4", "p3", "p7", "x1", "x5", "s0", "s4", "r2", "r6", "s1", "x2",
    "r3", "s5", "x6", "r7", "s2", "x3", "s6", "x7", "s3", "s7",
)


def kernel(
    q_ref, kv_ref, doc_ref, res_ref, w_ref, ids_ref, prio_ref,
    hid_out, rows_ref,
    hid_ref, qbuf, kvbuf, vt, mx, acc, att, wbuf, res, ids, prio, docs, mt, mtbuf, sel, psend, prec,
    xbuf, asend,
    in_s, kvu_s, kvu_r, kvy_s, kvy_r, q_s, q_r, w_s, w_r, ws_s, ws_r, mt_s, mt_r,
    p_s, p_r, x_s, x_r, y_s, y_r, a_s, a_r, l_s,
):
    ctx = lax.axis_index("ctx")
    head = lax.axis_index("head")
    core = lax.axis_index("dp")
    z = ctx // 2
    ylo = ctx % 2
    me = ylo * 8 + head

    def at_z(k):
        return {"ctx": ((z + k + NZ) % NZ) * 2 + ylo}

    def at_plane(p):
        return {"ctx": z * 2 + p // 8, "head": p % 8}

    partner = {"ctx": z * 2 + (1 - ylo)}
    sibling = {"dp": 1 - core}
    kind = head % 2
    twin = {"head": head + 1 - 2 * kind}

    def remote(src, dst, s, r, to):
        return pltpu.make_async_remote_copy(
            src_ref=src, dst_ref=dst, send_sem=s, recv_sem=r, device_id=to, device_id_type=MESH
        )

    def wait_for(ref, sem):
        pltpu.make_async_copy(ref, ref, sem).wait()

    key_head = pl.multiple_of((head // KV_GROUP) * HEAD_DIM, HEAD_DIM)
    loads = [
        pltpu.make_async_copy(src, dst, in_s.at[i])
        for i, (src, dst) in enumerate(
            (
                (kv_ref.at[:, :, pl.ds(key_head, HEAD_DIM)], kvbuf.at[0, :, 0]),
                (q_ref, qbuf.at[0]),
                (w_ref, wbuf.at[0]),
                (ids_ref, ids),
                (prio_ref, prio),
                (doc_ref, docs),
                (res_ref, res),
            )
        )
    ]
    for copy in loads:
        copy.start()

    barrier = pltpu.get_barrier_semaphore()

    def greet_plane(j, c):
        pl.semaphore_signal(barrier, inc=1, device_id=at_plane((me + j) % PLANE), device_id_type=MESH)
        return c

    def greet_z(j, c):
        pl.semaphore_signal(barrier, inc=1, device_id=at_z(j), device_id_type=MESH)
        return c

    lax.fori_loop(1, PLANE, greet_plane, 0)
    lax.fori_loop(1, NZ, greet_z, 0)
    pl.semaphore_signal(barrier, inc=1, device_id=sibling, device_id_type=MESH)

    def make_slots():
        row16 = lax.broadcasted_iota(jnp.int32, (16, 128), 0)
        lane16 = lax.broadcasted_iota(jnp.int32, (16, 128), 1)
        expert = lax.broadcasted_iota(jnp.int32, (128, 16), 0)
        chosen = jnp.zeros((128, 16), jnp.float32)
        for k in range(TOPK):
            chosen = chosen + jnp.where(ids[k : k + 1, :] == expert, 1.0, 0.0)
        prio_row = jnp.zeros((16, 128), jnp.int32)
        prio_col = jnp.zeros((16, 128), jnp.int32)
        for u in range(16):
            prio_row = jnp.where(lane16 == u, prio[u], prio_row)
            prio_col = jnp.where(row16 == u, prio[u], prio_col)
        earlier = jnp.where(prio_col < prio_row, 1.0, 0.0)[:, :16]
        ranks = jnp.dot(
            chosen.astype(jnp.bfloat16), earlier.astype(jnp.bfloat16), preferred_element_type=jnp.float32
        )
        slots = jnp.where(chosen > 0.5, ranks + 1.0, 0.0)
        place = jnp.where(lane16 == row16 + 16 * z, 1.0, 0.0)
        mt[...] = jnp.dot(
            slots.astype(jnp.bfloat16), place.astype(jnp.bfloat16), preferred_element_type=jnp.float32
        )

    pl.semaphore_wait(barrier, PLANE - 1 + NZ - 1 + 1)

    def kv_up(r):
        src = kvbuf.at[0 if r < 3 else 2, kind, 0]
        return remote(src, kvbuf.at[r, kind, 0], kvu_s.at[r], kvu_r.at[r], at_z(2 - r % 2))

    def kv_sides(r):
        if r == 0:
            return [remote(kvbuf.at[r, :, 0], kvbuf.at[r, :, 1], kvy_s.at[r, 0], kvy_r.at[r, 0], partner)]
        part = kvbuf.at[r, kind, 0]
        return [
            remote(part, kvbuf.at[r, kind, 1], kvy_s.at[r, 0], kvy_r.at[r, 0], partner),
            remote(part, kvbuf.at[r, kind, 1], kvy_s.at[r, 1], kvy_r.at[r, 1], partner | twin),
            remote(part, part, kvy_s.at[r, 2], kvy_r.at[r, 2], twin),
        ]

    def w_rows(c):
        return pl.ds(pl.multiple_of(core * 512 + c * WROWS, WROWS), WROWS)

    def w_ring(s, c):
        up = s < 4 or (s == 7 and c >= WCH // 2)
        before = 3 if s == 7 and up else s - 1
        src = w_ref.at[w_rows(c), :] if s in (1, 4) else wbuf.at[before, w_rows(c), :]
        to = at_z(1 if up else -1)
        return remote(src, wbuf.at[s, w_rows(c), :], w_s.at[s, c], w_r.at[s, c], to)

    def w_side(s, c):
        part = wbuf.at[s, w_rows(c), :]
        return remote(part, part, ws_s.at[s, c], ws_r.at[s, c], sibling)

    def w_forward(first, k):
        s, c = first + k // WCH, k % WCH
        if first == 1 and s == 4:
            s, c = 7, c + WCH // 2
        w_ring(s, c).wait_recv()
        if s == 3 and c >= WCH // 2 or s == 6 and c < WCH // 2:
            w_ring(7, c).start()
        elif s not in (3, 6, 7):
            w_ring(s + 1, c).start()
        w_side(s, c).start()

    q_swap = remote(qbuf.at[0], qbuf.at[1], q_s, q_r, partner)
    for c in range(WCH):
        w_ring(4, c).start()
    loads[0].wait()
    kv_up(1).start()
    kv_sides(0)[0].start()
    kv_up(2).start()
    loads[1].wait()
    q_swap.start()
    for copy in loads[3:]:
        copy.wait()
    make_slots()

    def mt_copy(j):
        to = (z + j) % NZ
        rows = pl.ds(pl.multiple_of(to * 16, 16), 16)
        return remote(mt.at[rows, :], mtbuf.at[z], mt_s, mt_r, at_z(j))

    def mt_send(j, c):
        mt_copy(j).start()
        return c

    lax.fori_loop(1, NZ, mt_send, 0)
    mtbuf[z] = mt[pl.ds(pl.multiple_of(z * 16, 16), 16), :]

    row = lax.broadcasted_iota(jnp.int32, (2 * ROWS, ROWS), 0)
    lane = lax.broadcasted_iota(jnp.int32, (1, ROWS), 1)

    def attend(r, w):
        yq = ylo if w == 0 else 1 - ylo
        last = r == REACH - 1
        key_pos = ((z - r + NZ) % NZ) * 256 + (row + ylo * ROWS) % 256
        keys = kvbuf[r, 0].reshape(2 * ROWS, HEAD_DIM)
        if w == 0:
            vt[r, :HEAD_DIM, :] = kvbuf[r, 1].reshape(2 * ROWS, HEAD_DIM).T
            vt[r, HEAD_DIM:, :] = jnp.ones((16, 2 * ROWS), jnp.bfloat16)
        pos = (2 * z + yq) * ROWS + lane
        start = jnp.zeros((1, ROWS), jnp.int32)
        end = jnp.int32(0)
        for d in range(DOCS):
            length = docs[d]
            end = end + length
            start = start + jnp.where(pos >= end, length, 0)
        bias = jnp.where((key_pos <= pos) & (key_pos >= start), 0.0, LOW)
        bias = jnp.concatenate([bias, bias], axis=1)
        for pair in range(HEADS_DEV // 2):
            b = w * (HEADS_DEV // 2) + pair
            first = pair * 2 * HEAD_DIM
            query = jnp.concatenate(
                [
                    qbuf[w, :, first : first + HEAD_DIM],
                    qbuf[w, :, first + HEAD_DIM : first + 2 * HEAD_DIM],
                ],
                axis=0,
            )
            s = lax.dot_general(
                keys, query, (((1,), (1,)), ((), ())), preferred_element_type=jnp.float32
            )
            s = s + bias
            new = jnp.max(s, axis=0, keepdims=True)
            if r > 0:
                old = mx[b]
                new = jnp.maximum(old, new)
            weight = jnp.exp2((s - new) * COEF).astype(jnp.bfloat16)
            out = jnp.dot(vt[r], weight, preferred_element_type=jnp.float32)
            if r > 0:
                out = out + acc[b] * jnp.exp2((old - new) * COEF)
            if not last:
                mx[b] = new
                acc[b] = out
            else:
                mixed = out[:HEAD_DIM] / out[HEAD_DIM : HEAD_DIM + 1]
                for i in range(2):
                    one = mixed[:, i * ROWS : (i + 1) * ROWS].T.astype(jnp.bfloat16)
                    att[w, :, first + i * HEAD_DIM : first + (i + 1) * HEAD_DIM] = one

    def kv_step(r):
        kv_up(r).wait_recv()
        if r == 2:
            kv_up(3).start()
            kv_up(4).start()
        for copy in kv_sides(r):
            copy.start()

    def kv_wait(r):
        for copy in kv_sides(r):
            copy.wait_recv()

    def w_begin(s):
        for c in range(WCH):
            w_ring(s, c).start()

    def p_copy(o, w, h):
        to = (ylo if w == 0 else 1 - ylo) * 8 + h
        rows = pl.ds(pl.multiple_of(h * 16, 16), 16)
        return remote(psend.at[o, w, rows, :], prec.at[o, me], p_s.at[o], p_r.at[o], at_plane(to))

    def project(o, sides=(0, 1)):
        if 0 in sides:
            if o == 0:
                loads[2].wait()
            else:
                for c in range(WCH):
                    w_side(o, c).wait_recv()
        count = len(sides) * ROWS
        left = att[...].reshape(count, 1024) if count == 2 * ROWS else att[sides[0]]
        part = jnp.dot(left, wbuf[o], preferred_element_type=jnp.float32).astype(jnp.bfloat16)
        for i, w in enumerate(sides):
            psend[o, w] = part[i * ROWS : (i + 1) * ROWS]
            if w == 0:
                prec[o, me] = psend[o, 0, pl.ds(pl.multiple_of(head * 16, 16), 16), :]

            def send(j, c, w=w):
                p_copy(o, w, (head + j) % 8).start()
                return c

            lax.fori_loop(1 - w, 8, send, 0, unroll=True)

    def make_selection():
        row16 = lax.broadcasted_iota(jnp.int32, (16, 128), 0)
        lane16 = lax.broadcasted_iota(jnp.int32, (16, 128), 1)
        wait_for(mtbuf.at[pl.ds(0, NZ - 1)], mt_r)
        table = mtbuf[0]
        for i in range(1, NZ):
            table = table + mtbuf[i]
        want = jnp.where(lane16 // 16 == row16 // 2, (row16 % 2 + 1).astype(jnp.float32), -1.0)
        for d in range(PLANE):
            hit = jnp.broadcast_to(table[d : d + 1, :], (16, 128)) == want
            sel[pl.ds(d * 16, 16), :] = jnp.where(hit, 1.0, 0.0).astype(jnp.bfloat16)

    def x_copy(o, k, far):
        part = xbuf.at[(z + k + NZ) % NZ, :, pl.ds(o * CW, CW)]
        if k == 0 and far in (2, -2):
            way = 0 if far > 0 else 1
            return remote(part, part, y_s.at[o, way], y_r.at[o, way], at_z(far))
        return remote(part, part, x_s.at[o], x_r.at[o], at_z(far))

    def x_passed(o):
        return ((-2, 1), (2, -1), (-2, 2) if o % 2 else (2, -2))

    def x_forward(o):
        x_copy(o, 0, 2).wait_recv()
        x_copy(o, 0, -2).wait_recv()
        for k, far in x_passed(o):
            x_copy(o, k, far).start()

    def reduce(o):
        wait_for(prec.at[o, pl.ds(0, PLANE - 1)], p_r.at[o])
        halves = []
        for side in range(2):
            total = jnp.zeros((16, 256), jnp.float32)
            for h in range(8):
                total = total + prec[o, side * 8 + h].astype(jnp.float32)
            halves.append(total)
        total = jnp.concatenate(halves, axis=1)
        cols = pl.ds(pl.multiple_of(((z + OFFSET[o] + NZ) % NZ) * CW, CW), CW)
        hidden = (res[:, cols].astype(jnp.float32) + total).astype(jnp.bfloat16)
        hid_ref[:, cols] = hidden
        xbuf[z, :, o * CW : (o + 1) * CW] = hidden

        for far in (2, -2, 1, -1):
            x_copy(o, 0, far).start()

    def a_copy(o, j):
        to = (me + j) % PLANE
        cols = pl.ds(o * CW, CW)
        return remote(asend.at[to, :, cols], rows_ref.at[me, :, cols], a_s.at[o], a_r.at[o], at_plane(to))

    def own_copy(o):
        cols = pl.ds(o * CW, CW)
        return pltpu.make_async_copy(asend.at[me, :, cols], rows_ref.at[me, :, cols], l_s.at[o])

    def select(o):
        wait_for(xbuf.at[pl.ds(0, 5), :, pl.ds(o * CW, CW)], x_r.at[o])
        cols = slice(o * CW, (o + 1) * CW)
        gathered = xbuf[:, :, cols].reshape(ROWS, CW)
        picked = jnp.dot(sel[...], gathered, preferred_element_type=jnp.float32)
        asend[:, :, cols] = picked.astype(jnp.bfloat16).reshape(PLANE, 16, CW)

        def send(j, c):
            a_copy(o, j).start()
            return c

        lax.fori_loop(1, PLANE, send, 0, unroll=True)
        own_copy(o).start()

    hid_copy = pltpu.make_async_copy(hid_ref, hid_out, l_s.at[NZ])

    steps = {
        "a": lambda r: attend(r, 0),
        "b": lambda r: attend(r, 1),
        "k": kv_step,
        "v": kv_wait,
        "q": lambda r: q_swap.wait_recv(),
        "i": w_begin,
        "D": lambda k: w_forward(4, k),
        "U": lambda k: w_forward(1, k),
        "p": project,
        "P": lambda o: project(o, (0,)),
        "Q": lambda o: project(o, (1,)),
        "m": lambda r: make_selection(),
        "r": reduce,
        "x": x_forward,
        "s": select,
    }
    for step in SCHEDULE:
        steps[step[0]](int(step[1:]))
    hid_copy.start()

    hid_copy.wait()
    for r in range(1, REACH):
        kv_up(r).wait_send()
    for r in range(REACH):
        for copy in kv_sides(r):
            copy.wait_send()
    q_swap.wait_send()
    for s in range(1, NZ):
        for c in range(WCH):
            w_ring(s, c).wait_send()
            w_side(s, c).wait_send()
    wait_for(mtbuf.at[pl.ds(0, NZ - 1)], mt_s)
    for o in range(NZ):
        wait_for(prec.at[o, pl.ds(0, PLANE - 1)], p_s.at[o])
        wait_for(xbuf.at[pl.ds(0, 5), :, pl.ds(o * CW, CW)], x_s.at[o])
        for far in (2, -2):
            x_copy(o, 0, far).wait_send()
        wait_for(asend.at[pl.ds(0, PLANE - 1), :, pl.ds(o * CW, CW)], a_s.at[o])
        own_copy(o).wait()
    for o in range(NZ):
        wait_for(asend.at[pl.ds(0, PLANE - 1), :, pl.ds(o * CW, CW)], a_r.at[o])


def finish(
    hid_ref, rows_ref, gain_ref, hid_out, rows_out, hid, rows, gain, wide_gain, out, sem
):
    ins = [pltpu.make_async_copy(gain_ref, gain, sem.at[0, 0]), pltpu.make_async_copy(hid_ref, hid, sem.at[0, 1])]
    for copy in ins:
        copy.start()
    to_hid = pltpu.make_async_copy(hid, hid_out, sem.at[1, 0])

    def row_in(p):
        return pltpu.make_async_copy(rows_ref.at[p], rows.at[p], sem.at[2, p])

    def row_out(p):
        return pltpu.make_async_copy(out.at[:, p], rows_out.at[:, p], sem.at[3, p])

    def begin(p, c):
        row_in(p).start()
        return c

    lax.fori_loop(0, PLANE, begin, 0)
    ins[0].wait()
    for k in range(NZ):
        for o in range(NZ):
            first = ((k + OFFSET[o]) % NZ) * CW
            part = jnp.broadcast_to(gain[:, first : first + CW], (2, CW))
            wide_gain[2 * k : 2 * k + 2, o * CW : (o + 1) * CW] = part
    ins[1].wait()
    to_hid.start()

    def one(p, c):
        row_in(p).wait()
        squares = jnp.zeros((16, CW), jnp.float32)
        for o in range(NZ):
            value = rows[p, :, o * CW : (o + 1) * CW].astype(jnp.float32)
            squares = squares + value * value
        scale = lax.rsqrt(jnp.sum(squares, axis=1, keepdims=True) / D + 1e-06)
        for o in range(NZ):
            cols = slice(o * CW, (o + 1) * CW)
            value = rows[p, :, cols].astype(jnp.float32) * scale * wide_gain[:, cols]
            value = value.astype(jnp.bfloat16).reshape(NZ, 2, CW)
            for k in range(NZ):
                first = ((k + OFFSET[o]) % NZ) * CW
                out[k, p, :, first : first + CW] = value[k]
        row_out(p).start()
        return c

    lax.fori_loop(0, PLANE, one, 0)

    def end(p, c):
        row_out(p).wait()
        return c

    lax.fori_loop(0, PLANE, end, 0)
    to_hid.wait()


def local(queries, keys_values, doc_lengths, residual, out_weight, norm_gain, expert_ids, priority):
    anywhere = pl.BlockSpec(memory_space=pl.ANY)
    bf16, f32 = jnp.bfloat16, jnp.float32
    dma = pltpu.SemaphoreType.DMA
    wide_gain = norm_gain.reshape(1, D)
    hidden, rows = pl.pallas_call(
        kernel,
        out_shape=(
            jax.ShapeDtypeStruct((16, D), bf16),
            jax.ShapeDtypeStruct((PLANE, 16, D), bf16),
        ),
        in_specs=[anywhere] * 7,
        out_specs=(anywhere, anywhere),
        scratch_shapes=[
            pltpu.VMEM((16, D), bf16),
            pltpu.VMEM((2, ROWS, 1024), bf16),
            pltpu.VMEM((REACH, 2, 2, ROWS, HEAD_DIM), bf16),
            pltpu.VMEM((REACH, HEAD_DIM + 16, 2 * ROWS), bf16),
            pltpu.VMEM((HEADS_DEV, 1, 2 * ROWS), f32),
            pltpu.VMEM((HEADS_DEV, HEAD_DIM + 16, 2 * ROWS), f32),
            pltpu.VMEM((2, ROWS, 1024), bf16),
            pltpu.VMEM((NZ, 1024, 256), bf16),
            pltpu.VMEM((16, D), bf16),
            pltpu.VMEM((TOPK, 16), jnp.int32),
            pltpu.SMEM((16,), jnp.int32),
            pltpu.SMEM((DOCS,), jnp.int32),
            pltpu.VMEM((128, 128), f32),
            pltpu.VMEM((NZ, 16, 128), f32),
            pltpu.VMEM((256, 128), bf16),
            pltpu.VMEM((NZ, 2, ROWS, 256), bf16),
            pltpu.VMEM((NZ, PLANE, 16, 256), bf16),
            pltpu.VMEM((NZ, 16, D), bf16),
            pltpu.VMEM((PLANE, 16, D), bf16),
            dma((7,)),
            dma((REACH,)), dma((REACH,)), dma((REACH, 3)), dma((REACH, 3)),
            dma(()), dma(()),
            dma((NZ, WCH)), dma((NZ, WCH)), dma((NZ, WCH)), dma((NZ, WCH)),
            dma(()), dma(()),
            dma((NZ,)), dma((NZ,)),
            dma((NZ,)), dma((NZ,)), dma((NZ, 2)), dma((NZ, 2)),
            dma((NZ,)), dma((NZ,)), dma((NZ + 1,)),
        ],
        compiler_params=pltpu.CompilerParams(
            collective_id=0, has_side_effects=True, vmem_limit_bytes=62 * 1024 * 1024
        ),
    )(
        queries, keys_values, doc_lengths, residual, out_weight,
        expert_ids.T, priority,
    )
    hidden, rows = pl.pallas_call(
        finish,
        out_shape=(
            jax.ShapeDtypeStruct((16, D), bf16),
            jax.ShapeDtypeStruct((NZ, PLANE, 2, D), bf16),
        ),
        in_specs=[anywhere] * 3,
        out_specs=(anywhere, anywhere),
        scratch_shapes=[
            pltpu.VMEM((16, D), bf16),
            pltpu.VMEM((PLANE, 16, D), bf16),
            pltpu.VMEM((1, D), f32),
            pltpu.VMEM((16, D), f32),
            pltpu.VMEM((NZ, PLANE, 2, D), bf16),
            dma((4, PLANE)),
        ],
        compiler_params=pltpu.CompilerParams(vmem_limit_bytes=62 * 1024 * 1024),
    )(hidden, rows, wide_gain)
    return hidden, rows.reshape(1, PLANE * NZ, 2, D)


def solution(mesh):
    return jax.shard_map(
        local,
        mesh=mesh,
        in_specs=(
            P(("dp", "ctx"), "head"),
            P(None, ("dp", "ctx"), None),
            P("dp"),
            P(("dp", "ctx", "head"), None),
            P("head", "ctx"),
            P(),
            P(("dp", "ctx", "head"), None),
            P(("dp", "ctx", "head")),
        ),
        out_specs=(P(("dp", "ctx", "head"), None), P(("ctx", "head"), "dp", None, None)),
        check_vma=False,
    )
```
